512 devices in a mesh: section: 32 (over y, z_lo), dp: 16 (over z_hi, x, core).
Axes of the slice: x: 4, y: 4, z: 16 (z_hi: 2, z_lo: 8; z = z_hi * 8 + z_lo), core: 2. Of those that a mesh axis runs over, the one named last changes fastest.
Arguments:
- acts: bfloat16 [32, 2, 1024, 6144], P('section', None, 'dp'), may hold values from -6 to 6
- grads_sent: bfloat16 [32, 2, 1024, 6144], P('section', None, 'dp'), may hold values from -48 to 48
- replicas: bfloat16 [32, 2, 2, 16, 6144], P('section'), may hold values from -4 to 4
- master: float32 [32, 2, 16, 6144], P('section', None, None, 'dp'), may hold values from -1 to 1
- moment: float32 [32, 2, 16, 6144], P('section', None, None, 'dp'), may hold values from -3 to 3
- second: float32 [32, 2, 16, 6144], P('section', None, None, 'dp'), may hold values from 0.05 to 4
Outputs:
- new_master: float32 [32, 2, 16, 6144], P('section', None, None, 'dp')
- new_moment: float32 [32, 2, 16, 6144], P('section', None, None, 'dp')
- new_second: float32 [32, 2, 16, 6144], P('section', None, None, 'dp')
- new_replicas: bfloat16 [32, 2, 2, 16, 6144], P('section')
The draws below stay inside these ranges and needn't reach their ends.
All inputs are finite; a program needn't handle non-finite values.
Results may differ from the reference program's by a relative error of at most 0.006.
Values may be sent and summed in bfloat16 or wider, within the bound.
No kernel may reach another device: no remote copies, remote signals or barrier semaphores. Data moves between devices by JAX's collectives and lax.ppermute only.
A program may use at most 64 MiB of HBM per device.

```python
import math
import jax
import jax.numpy as jnp
from jax import lax

D = 6144
FF = 24576
UNITS = 16
TOKENS = 1024
N_SECTION = 32


def block_scale(rng, shape, pieces, low, top_value):
    loudness = 1.0
    for axis_at, blocks in pieces:
        steps = jax.random.uniform(jax.random.fold_in(jax.random.fold_in(rng, 6), axis_at), (blocks,), jnp.float32, low / len(pieces), top_value / len(pieces))
        loudness = loudness * jnp.repeat(jnp.exp(steps), shape[axis_at] // blocks).reshape((-1,) + (1,) * (len(shape) - 1 - axis_at))
    return loudness


def gaussian(stream_key, extent, width, bound, cuts=(), held_as=jnp.bfloat16):
    values = width * jax.random.normal(stream_key, extent, jnp.float32)
    if cuts:
        values = values * block_scale(stream_key, extent, cuts, -0.22, 0.18)
    return jnp.clip(values, -bound, bound).astype(held_as)


def setup_inputs(seed: int = 0) -> dict:
    arg_keys = jax.random.split(jax.random.key(seed), 7)
    acts = gaussian(arg_keys[0], (N_SECTION, 2, TOKENS, D), 1.0, 6.0, ((0, 32), (2, 16)))
    grads_sent = gaussian(arg_keys[1], (N_SECTION, 2, TOKENS, D), 8.0, 48.0, ((0, 32), (2, 16)))
    replicas = gaussian(arg_keys[2], (N_SECTION, 2, 2, UNITS, D), 1.0, 4.0, ((0, 32),))
    master = gaussian(arg_keys[3], (N_SECTION, 2, UNITS, D), 0.25, 1.0, ((0, 32), (3, 16)), jnp.float32)
    moment = gaussian(arg_keys[4], (N_SECTION, 2, UNITS, D), 0.5, 3.0, ((0, 32), (3, 16)), jnp.float32)
    second = jnp.clip(jnp.exp(math.log(4.0) - 4.3820266 * jax.random.uniform(arg_keys[5], (N_SECTION, 2, UNITS, D), jnp.float32) ** block_scale(arg_keys[5], (N_SECTION, 2, UNITS, D), ((0, 32), (3, 16)), -0.2, 0.2)), 0.05, 4.0)
    return {"acts": acts, "grads_sent": grads_sent, "replicas": replicas, "master": master, "moment": moment, "second": second}


def gelu_exact(values):
    return 0.5 * values * (1.0 + lax.erf(values * 0.7071067811865476))

def gelu_slope(values):
    return 0.5 * (1.0 + lax.erf(values * 0.7071067811865476)) + values * jnp.exp(-0.5 * values * values) * 0.3989422804014327

def section_terms(inputs, upstream, w_in, w_out):
    inv_width = 1.0 / D ** 0.5
    inv_hidden = 1.0 / FF ** 0.5
    pre_act = jnp.dot(inputs, w_in.T, preferred_element_type=jnp.float32) * inv_width
    activation = gelu_exact(pre_act).astype(jnp.bfloat16)
    act_grad = jnp.dot(upstream, w_out.T, preferred_element_type=jnp.float32) * inv_hidden
    pre_grad = (act_grad * gelu_slope(pre_act)).astype(jnp.bfloat16)
    term_in = jnp.dot(pre_grad.T, inputs, preferred_element_type=jnp.float32) * inv_width
    term_out = jnp.dot(activation.T, upstream, preferred_element_type=jnp.float32) * inv_hidden
    return jnp.stack([term_in, term_out])

def reference(acts, grads_sent, replicas, master, moment, second):
    sections = N_SECTION

    def per_worker(worker):
        after = (worker + 1) % sections
        before = (worker + sections - 1) % sections
        down_up = lax.dynamic_index_in_dim(grads_sent, after.astype(jnp.int32), 0, keepdims=False)[0]
        up_up = lax.dynamic_index_in_dim(grads_sent, before.astype(jnp.int32), 0, keepdims=False)[1]
        own_acts = lax.dynamic_index_in_dim(acts, worker.astype(jnp.int32), 0, keepdims=False)
        own_weights = lax.dynamic_index_in_dim(replicas, worker.astype(jnp.int32), 0, keepdims=False)
        down_terms = section_terms(own_acts[0], down_up, own_weights[0, 0], own_weights[0, 1])
        up_terms = section_terms(own_acts[1], up_up, own_weights[1, 0], own_weights[1, 1])
        return jnp.stack([down_terms, up_terms])
    workers = jnp.arange(sections, dtype=jnp.int32)
    terms = lax.map(per_worker, workers)
    grad = terms[:, 0] + terms[::-1, 1]
    owner_proj = (workers >= sections // 2).astype(jnp.int32)
    mirrors = (sections - 1 - workers).astype(jnp.int32)
    owned = jnp.stack([grad[workers, owner_proj], grad[mirrors, owner_proj]], axis=1)
    new_moment = 0.9 * moment + 0.1 * owned
    new_second = 0.95 * second + 0.05 * owned * owned
    corrected = new_moment / (1.0 - 0.9 ** 10) / (jnp.sqrt(new_second / (1.0 - 0.95 ** 10)) + 1e-08)
    new_master = master - 0.05 * (corrected + 0.01 * master)
    lower = jnp.minimum(workers, mirrors)
    higher = jnp.maximum(workers, mirrors)
    lower_slot = jnp.where(lower == workers, 0, 1).astype(jnp.int32)
    higher_slot = jnp.where(higher == workers, 0, 1).astype(jnp.int32)
    full_section = jnp.stack([new_master[lower, lower_slot], new_master[higher, higher_slot]], axis=1)
    new_replicas = jnp.stack([full_section, full_section[::-1]], axis=1).astype(jnp.bfloat16)
    return (new_master, new_moment, new_second, new_replicas)
```

```python
import jax
import jax.numpy as jnp
from jax import lax
from jax.sharding import Mesh, PartitionSpec as P

D = 6144
FF = 24576

beta_one = 0.9
beta_two = 0.95
adam_eps = 1e-08
learn_rate = 0.05
decay_rate = 0.01
adam_steps = 10.0

SECTION = ("y", "zl")
DP = ("zh", "x", "c")
NEAR = ("x", "c")
FAR = ("y", "zl", "zh")


def far_groups():
    groups = []
    for low in range(16):
        groups.append([w * 2 + zh for w in (low, 31 - low) for zh in range(2)])
    return groups


def shifted(block, distance):
    route = [((i - distance) % 32, i) for i in range(32)]
    return lax.ppermute(block, SECTION, route)


def gelu_exact(values):
    return 0.5 * values * (1.0 + lax.erf(values * 0.7071067811865476))


def gelu_slope(values):
    return (
        0.5 * (1.0 + lax.erf(values * 0.7071067811865476))
        + values * jnp.exp(-0.5 * values * values) * 0.3989422804014327
    )


def dot(a, b, ca, cb):
    return lax.dot_general(a, b, (((ca,), (cb,)), ((), ())), preferred_element_type=jnp.float32)


def terms_of(inputs, upstream, w_in, w_out):
    inv_width = 1.0 / D**0.5
    inv_hidden = 1.0 / FF**0.5
    pre_act = dot(w_in, inputs, 1, 1) * inv_width
    activation = gelu_exact(pre_act).astype(jnp.bfloat16)
    act_grad = dot(w_out, upstream, 1, 1) * inv_hidden
    pre_grad = (act_grad * gelu_slope(pre_act)).astype(jnp.bfloat16)
    term_in = dot(pre_grad, inputs, 1, 0) * inv_width
    term_out = dot(activation, upstream, 1, 0) * inv_hidden
    return jnp.stack([term_in, term_out])


def body(acts, grads_sent, replicas, master, moment, second):
    upper = lax.axis_index("y") >= 2
    from_after = shifted(grads_sent[0, 0], -1)
    from_before = shifted(grads_sent[0, 1], 1)
    down = terms_of(acts[0, 0], from_after, replicas[0, 0, 0], replicas[0, 0, 1])
    up = terms_of(acts[0, 1], from_before, replicas[0, 1, 0], replicas[0, 1, 1])
    pair = jnp.stack(
        [jnp.where(upper, up, down), jnp.where(upper, down, up)], axis=1
    ).astype(jnp.bfloat16)
    tiles = pair.reshape(2, 2, 16, 2, 8, 384).transpose(4, 0, 3, 1, 2, 5)
    near = lax.all_to_all(tiles, NEAR, 0, 0, tiled=True)
    near = near.astype(jnp.float32).sum(axis=0).astype(jnp.bfloat16)
    far = lax.all_to_all(
        near.reshape(4, 2, 16, 384), FAR, 0, 0, axis_index_groups=far_groups(), tiled=True
    )
    summed = far.astype(jnp.float32).sum(axis=0)
    grads = jnp.where(upper, summed[::-1], summed)
    moment_now = beta_one * moment[0] + (1.0 - beta_one) * grads
    second_now = beta_two * second[0] + (1.0 - beta_two) * grads * grads
    corrected = (
        moment_now
        / (1.0 - beta_one**adam_steps)
        / (jnp.sqrt(second_now / (1.0 - beta_two**adam_steps)) + adam_eps)
    )
    master_now = master[0] - learn_rate * (corrected + decay_rate * master[0])
    rounded = master_now.astype(jnp.bfloat16)
    rounded = jnp.where(upper, rounded[::-1], rounded)
    shared = lax.all_to_all(
        jnp.broadcast_to(rounded[None], (4, 2, 16, 384)),
        FAR, 0, 0, axis_index_groups=far_groups(), tiled=True,
    )
    full = lax.all_gather(shared, NEAR, axis=0, tiled=False)
    full = full.reshape(8, 2, 2, 2, 16, 384).transpose(3, 1, 4, 2, 0, 5).reshape(2, 2, 16, D)
    new_replicas = jnp.where(upper, full[::-1], full)
    return (master_now[None], moment_now[None], second_now[None], new_replicas[None])


def solution(mesh):
    fine = Mesh(mesh.devices.reshape(4, 8, 2, 4, 2), ("y", "zl", "zh", "x", "c"))
    in_specs = (
        P(SECTION, None, DP, None),
        P(SECTION, None, DP, None),
        P(SECTION, None, None, None, None),
        P(SECTION, None, None, DP),
        P(SECTION, None, None, DP),
        P(SECTION, None, None, DP),
    )
    out_specs = (
        P(SECTION, None, None, DP),
        P(SECTION, None, None, DP),
        P(SECTION, None, None, DP),
        P(SECTION, None, None, None, None),
    )
    return jax.shard_map(body, mesh=fine, in_specs=in_specs, out_specs=out_specs, check_vma=False)
```

```python
import functools

import jax
import jax.numpy as jnp
from jax import lax
from jax.experimental import pallas as pl
from jax.experimental.pallas import tpu as pltpu
from jax.sharding import Mesh, PartitionSpec as P

D = 6144
FF = 24576

beta_one = 0.9
beta_two = 0.95
adam_eps = 1e-08
learn_rate = 0.05
decay_rate = 0.01
adam_steps = 10.0

SECTION = ("y", "zl")
DP = ("zh", "x", "c")
NEAR = ("x", "c")
FAR = ("y", "zl", "zh")


def far_groups():
    groups = []
    for low in range(16):
        groups.append([w * 2 + zh for w in (low, 31 - low) for zh in range(2)])
    return groups


def far_index(w, zh):
    return (w % 32) * 2 + zh


def wrap_route(flip):
    route = []
    for w in range(7, 32, 8):
        for zh in range(2):
            left, right = far_index(w, zh), far_index(w + 1, zh ^ flip)
            route += [(left, right), (right, left)]
    return route


def shifted(block, distance):
    skipped = 7 if distance < 0 else 0
    route = [((i - distance) % 32, i) for i in range(32) if i % 8 != skipped]
    return lax.ppermute(block, SECTION, route)


def take_kernel(c, src, dst, sem):
    copy = pltpu.make_async_copy(src.at[0, c], dst, sem)
    copy.start()
    copy.wait()


def take(array, c):
    shape = array.shape[2:]
    return pl.pallas_call(
        functools.partial(take_kernel, c),
        out_shape=jax.ShapeDtypeStruct(shape, array.dtype),
        in_specs=[pl.BlockSpec(memory_space=pl.ANY)],
        out_specs=pl.BlockSpec(memory_space=pl.ANY),
        scratch_shapes=[pltpu.SemaphoreType.DMA],
    )(array)


def gelu_exact(values):
    return 0.5 * values * (1.0 + lax.erf(values * 0.7071067811865476))


def gelu_slope(values):
    return (
        0.5 * (1.0 + lax.erf(values * 0.7071067811865476))
        + values * jnp.exp(-0.5 * values * values) * 0.3989422804014327
    )


def dot(a, b, ca, cb):
    return lax.dot_general(a, b, (((ca,), (cb,)), ((), ())), preferred_element_type=jnp.float32)


def body(acts, grads_sent, replicas, master, moment, second):
    inv_width = 1.0 / D**0.5
    inv_hidden = 1.0 / FF**0.5
    upper = lax.axis_index("y") >= 2
    zl = lax.axis_index("zl")
    left, right = zl == 7, zl == 0
    w_outs = lax.ppermute(
        jnp.where(left, replicas[0, 0, 1], replicas[0, 1, 1]), FAR, wrap_route(1)
    )
    upstream = [shifted(take(grads_sent, 0), -1), shifted(take(grads_sent, 1), 1)]
    pre_act = [dot(replicas[0, c, 0], acts[0, c], 1, 1) * inv_width for c in range(2)]
    held = jnp.where(left, grads_sent[0, 1], grads_sent[0, 0])
    wrap_grad = dot(w_outs, held, 1, 1) * inv_hidden
    sent = jnp.concatenate([jnp.where(left, pre_act[0], pre_act[1]), wrap_grad], axis=0)
    wrapped = lax.ppermute(sent, FAR, wrap_route(0))
    terms = []
    for c, wrap in enumerate((left, right)):
        act_grad = dot(replicas[0, c, 1], upstream[c], 1, 1) * inv_hidden
        act_grad = jnp.where(wrap, wrapped[16:], act_grad)
        pre_grad = (act_grad * gelu_slope(pre_act[c])).astype(jnp.bfloat16)
        activation = gelu_exact(jnp.where(wrap, wrapped[:16], pre_act[c])).astype(jnp.bfloat16)
        term_in = dot(pre_grad, acts[0, c], 1, 0) * inv_width
        term_out = dot(activation, jnp.where(wrap, held, upstream[c]), 1, 0) * inv_hidden
        terms.append(jnp.stack([term_in, term_out]).astype(jnp.bfloat16))
    tiles = jnp.stack(terms).reshape(2, 2, 16, 2, 8, 384).transpose(4, 0, 1, 3, 2, 5)
    near = lax.all_to_all(tiles, NEAR, 0, 0, tiled=True)
    near = near.astype(jnp.float32).sum(axis=0).astype(jnp.bfloat16)
    down, up = near[0], near[1]
    other = lax.ppermute(jnp.where(left, down[1], up[1]), FAR, wrap_route(1))
    down = jnp.stack([down[0], jnp.where(left, other, down[1])])
    up = jnp.stack([up[0], jnp.where(right, other, up[1])])
    near = jnp.stack([jnp.where(upper, up, down), jnp.where(upper, down, up)], axis=2)
    far = lax.all_to_all(
        near.reshape(4, 2, 16, 384), FAR, 0, 0, axis_index_groups=far_groups(), tiled=True
    )
    summed = far.astype(jnp.float32).sum(axis=0)
    grads = jnp.where(upper, summed[::-1], summed)
    moment_now = beta_one * moment[0] + (1.0 - beta_one) * grads
    second_now = beta_two * second[0] + (1.0 - beta_two) * grads * grads
    corrected = (
        moment_now
        / (1.0 - beta_one**adam_steps)
        / (jnp.sqrt(second_now / (1.0 - beta_two**adam_steps)) + adam_eps)
    )
    master_now = master[0] - learn_rate * (corrected + decay_rate * master[0])
    rounded = master_now.astype(jnp.bfloat16)
    rounded = jnp.where(upper, rounded[::-1], rounded)
    shared = lax.all_to_all(
        jnp.broadcast_to(rounded[None], (4, 2, 16, 384)),
        FAR, 0, 0, axis_index_groups=far_groups(), tiled=True,
    )
    full = lax.all_gather(shared, NEAR, axis=0, tiled=False)
    full = full.reshape(8, 2, 2, 2, 16, 384).transpose(3, 1, 4, 2, 0, 5).reshape(2, 2, 16, D)
    new_replicas = jnp.where(upper, full[::-1], full)
    return (master_now[None], moment_now[None], second_now[None], new_replicas[None])


def solution(mesh):
    fine = Mesh(mesh.devices.reshape(4, 8, 2, 4, 2), ("y", "zl", "zh", "x", "c"))
    in_specs = (
        P(SECTION, None, DP, None),
        P(SECTION, None, DP, None),
        P(SECTION, None, None, None, None),
        P(SECTION, None, None, DP),
        P(SECTION, None, None, DP),
        P(SECTION, None, None, DP),
    )
    out_specs = (
        P(SECTION, None, None, DP),
        P(SECTION, None, None, DP),
        P(SECTION, None, None, DP),
        P(SECTION, None, None, None, None),
    )
    return jax.shard_map(body, mesh=fine, in_specs=in_specs, out_specs=out_specs, check_vma=False)
```

```python
import functools

import jax
import jax.numpy as jnp
from jax import lax
from jax.experimental import pallas as pl
from jax.experimental.pallas import tpu as pltpu
from jax.sharding import Mesh, PartitionSpec as P

D = 6144
FF = 24576
UNITS = 16
INV_WIDTH = 1.0 / D**0.5
INV_HIDDEN = 1.0 / FF**0.5

beta_one = 0.9
beta_two = 0.95
adam_eps = 1e-08
learn_rate = 0.05
decay_rate = 0.01
adam_steps = 10.0

SECTION = ("y", "zl")
DP = ("zh", "x", "c")
NEAR = ("x", "c")
FAR = ("y", "zl", "zh")

ANY = pl.BlockSpec(memory_space=pl.ANY)
VMEM = pl.BlockSpec(memory_space=pltpu.VMEM)
BF16 = jnp.bfloat16
F32 = jnp.float32


def far_groups():
    groups = []
    for low in range(16):
        groups.append([w * 2 + zh for w in (low, 31 - low) for zh in range(2)])
    return groups


def wrap_route():
    route = []
    for left in range(7, 32, 8):
        right = (left + 1) % 32
        route += [(left, right), (right, left)]
    return route


def swap_route():
    return [(7, 23), (23, 7), (8, 24), (24, 8)]


def weights_route():
    route = []
    for w, v in wrap_route():
        for zh in range(2):
            route.append((w * 2 + zh, v * 2 + 1 - zh))
    return route


def shifted(block, distance):
    skipped = 7 if distance < 0 else 0
    route = [((i - distance) % 32, i) for i in range(32) if i % 8 != skipped]
    return lax.ppermute(block, SECTION, route)


def swap_cores(block):
    return lax.ppermute(block, "c", [(0, 1), (1, 0)])


def here(array):
    return pltpu.with_memory_space_constraint(array, pltpu.VMEM)


def call(kernel, outs, *args, specs=None, scratch=(), flops=0, moved=0):
    return pl.pallas_call(
        kernel,
        out_shape=[pltpu.VMEM(*out) if isinstance(out, tuple) else out for out in outs],
        in_specs=specs or [VMEM] * len(args),
        out_specs=[VMEM if isinstance(out, tuple) else ANY for out in outs],
        scratch_shapes=list(scratch),
        cost_estimate=pl.CostEstimate(flops=flops, bytes_accessed=moved, transcendentals=0),
        compiler_params=pltpu.CompilerParams(vmem_limit_bytes=32 * 2**20),
    )(*args)


def gelu_exact(values):
    return 0.5 * values * (1.0 + lax.erf(values * 0.7071067811865476))


def gelu_slope(values):
    return (
        0.5 * (1.0 + lax.erf(values * 0.7071067811865476))
        + values * jnp.exp(-0.5 * values * values) * 0.3989422804014327
    )


def dot(a, b, ca, cb):
    return lax.dot_general(a, b, (((ca,), (cb,)), ((), ())), preferred_element_type=F32)


def take_kernel(grads, weights, w_out, down, up, sems):
    side = jnp.where(lax.axis_index("zl") == 7, 0, 1)
    copies = [
        pltpu.make_async_copy(weights.at[0, side, 1], w_out, sems.at[0]),
        pltpu.make_async_copy(grads.at[0, 0], down, sems.at[1]),
        pltpu.make_async_copy(grads.at[0, 1], up, sems.at[2]),
    ]
    for copy in copies:
        copy.start()
    for copy in copies:
        copy.wait()


def forward_kernel(acts, weights, pre_act):
    for c in range(2):
        pre_act[c] = dot(weights[0, c, 0], acts[0, c], 1, 1) * INV_WIDTH


def wrap_kernel(w_out, down, up, pre_act, sent):
    left = lax.axis_index("zl") == 7

    @pl.when(left)
    def _():
        sent[:UNITS] = pre_act[0]
        sent[UNITS:] = dot(w_out[...], up[...], 1, 1) * INV_HIDDEN

    @pl.when(jnp.logical_not(left))
    def _():
        sent[:UNITS] = pre_act[1]
        sent[UNITS:] = dot(w_out[...], down[...], 1, 1) * INV_HIDDEN


def terms_kernel(
    from_after, from_before, wrapped, acts, weights, pre_act, down, up, keep, send, grad, factor
):
    zl = lax.axis_index("zl")
    first = lax.axis_index("c") == 0

    def product(lhs, rhs, scale, row):
        for block in range(8):
            x, zh = block % 4, block // 4
            even = dot(lhs, rhs(block * 768), 1, 0) * scale
            odd = dot(lhs, rhs(block * 768 + 384), 1, 0) * scale
            spot = (x, pl.ds(row, UNITS), pl.ds(zh * 384, 384))
            keep[spot] = jnp.where(first, even, odd)
            send[spot] = jnp.where(first, odd, even).astype(BF16)

    for c in range(2):
        wrap = zl == (7 if c == 0 else 0)
        upstream = from_after if c == 0 else from_before
        own = up if c == 0 else down

        @pl.when(wrap)
        def _():
            grad[...] = wrapped[UNITS:]
            factor[...] = wrapped[:UNITS]

        @pl.when(jnp.logical_not(wrap))
        def _():
            grad[...] = dot(weights[0, c, 1], upstream[...], 1, 1) * INV_HIDDEN
            factor[...] = pre_act[c]

        pre_grad = (grad[...] * gelu_slope(pre_act[c])).astype(BF16)
        activation = gelu_exact(factor[...]).astype(BF16)
        row = c * 2 * UNITS
        product(pre_grad, lambda at: acts[0, c, :, at : at + 384], INV_WIDTH, row)

        @pl.when(wrap)
        def _():
            product(activation, lambda at: own[:, at : at + 384], INV_HIDDEN, row + UNITS)

        @pl.when(jnp.logical_not(wrap))
        def _():
            product(activation, lambda at: upstream[:, at : at + 384], INV_HIDDEN, row + UNITS)


def merge_kernel(keep, arrived, out):
    out[...] = (keep[...] + arrived[...].astype(F32)).astype(BF16)


def near_kernel(arrived, total, swap):
    for row in range(4):
        rows = pl.ds(row * UNITS, UNITS)
        part = arrived[0, rows].astype(F32)
        for x in range(1, 4):
            part += arrived[x, rows].astype(F32)
        total[rows] = part.astype(BF16)
    side = jnp.where(lax.axis_index("zl") == 7, UNITS, 3 * UNITS)
    swap[...] = total[pl.ds(pl.multiple_of(side, UNITS), UNITS)]


def spread_kernel(total, swap, out):
    y, zl = lax.axis_index("y"), lax.axis_index("zl")
    upper = y >= 2
    for zh in range(2):
        columns = slice(zh * 384, zh * 384 + 384)
        for p in range(2):
            parts = []
            for c in range(2):
                part = total[(2 * c + p) * UNITS : (2 * c + p + 1) * UNITS, columns]
                if p == 1:
                    moved = (zl == (7 if c == 0 else 0)) & (y % 2 == c)
                    part = jnp.where(moved, swap[:, columns], part)
                parts.append(part)
            out[2 * p + zh, 0] = jnp.where(upper, parts[1], parts[0])
            out[2 * p + zh, 1] = jnp.where(upper, parts[0], parts[1])


def adam_kernel(arrived, master, moment, second, new_master, new_moment, new_second, shared):
    upper = lax.axis_index("y") >= 2
    sums = []
    for sec in range(2):
        part = arrived[0, sec].astype(F32)
        for i in range(1, 4):
            part += arrived[i, sec].astype(F32)
        sums.append(part)
    rounded = []
    for j in range(2):
        grad = jnp.where(upper, sums[1 - j], sums[j])
        moment_now = beta_one * moment[0, j] + (1.0 - beta_one) * grad
        second_now = beta_two * second[0, j] + (1.0 - beta_two) * grad * grad
        corrected = (
            moment_now
            / (1.0 - beta_one**adam_steps)
            / (jnp.sqrt(second_now / (1.0 - beta_two**adam_steps)) + adam_eps)
        )
        old = master[0, j]
        master_now = old - learn_rate * (corrected + decay_rate * old)
        new_master[0, j] = master_now
        new_moment[0, j] = moment_now
        new_second[0, j] = second_now
        rounded.append(master_now.astype(BF16))
    for sec in range(2):
        part = jnp.where(upper, rounded[1 - sec], rounded[sec])
        for i in range(4):
            shared[i, sec] = part


def finish_kernel(full, out, sem):
    upper = jnp.where(lax.axis_index("y") >= 2, 1, 0)
    copies = []
    for near in range(8):
        for zh in range(2):
            for sec in range(2):
                c = sec + upper - 2 * sec * upper
                at = (zh * 8 + near) * 384
                for p in range(2):
                    copies.append(
                        pltpu.make_async_copy(
                            full.at[near, 2 * p + zh, sec], out.at[0, c, p, :, pl.ds(at, 384)], sem
                        )
                    )
    for copy in copies:
        copy.start()
    for copy in copies:
        copy.wait()


def body(acts, grads_sent, replicas, master, moment, second):
    acts, weights = here(acts), here(replicas)
    w_out, down, up = call(
        take_kernel,
        [((UNITS, D), BF16), ((64, D), BF16), ((64, D), BF16)],
        grads_sent, replicas, specs=[ANY, ANY], scratch=[pltpu.SemaphoreType.DMA((3,))],
    )
    w_out = lax.ppermute(w_out, FAR, weights_route())
    from_after, from_before = shifted(down, -1), shifted(up, 1)
    (pre_act,) = call(forward_kernel, [((2, UNITS, 64), F32)], acts, weights)
    (sent,) = call(wrap_kernel, [((2 * UNITS, 64), F32)], here(w_out), down, up, pre_act)
    wrapped = lax.ppermute(sent, SECTION, wrap_route())
    keep, send = call(
        terms_kernel,
        [((4, 64, 768), F32), ((4, 64, 768), BF16)],
        here(from_after), here(from_before), here(wrapped), acts, weights, pre_act, down, up,
        scratch=[pltpu.VMEM((UNITS, 64), F32), pltpu.VMEM((UNITS, 64), F32)],
    )
    arrived = swap_cores(send)
    (tiles,) = call(merge_kernel, [((4, 64, 768), BF16)], keep, here(arrived))
    near = lax.all_to_all(tiles, "x", 0, 0, tiled=True)
    total, swap = call(near_kernel, [((64, 768), BF16), ((UNITS, 768), BF16)], here(near))
    swap = lax.ppermute(swap, SECTION, swap_route())
    (spread,) = call(spread_kernel, [((4, 2, UNITS, 384), BF16)], total, here(swap))
    far = lax.all_to_all(spread, FAR, 0, 0, axis_index_groups=far_groups(), tiled=True)
    shard = ((1, 2, UNITS, 384), F32)
    new_master, new_moment, new_second, shared = call(
        adam_kernel,
        [shard, shard, shard, ((4, 2, UNITS, 384), BF16)],
        here(far), here(master), here(moment), here(second),
    )
    shared = lax.all_to_all(shared, FAR, 0, 0, axis_index_groups=far_groups(), tiled=True)
    full = lax.all_gather(shared, NEAR, axis=0, tiled=False)
    (new_replicas,) = call(
        finish_kernel,
        [jax.ShapeDtypeStruct((1, 2, 2, UNITS, D), BF16)],
        here(full), scratch=[pltpu.SemaphoreType.DMA],
    )
    return (new_master, new_moment, new_second, new_replicas)


def solution(mesh):
    fine = Mesh(mesh.devices.reshape(4, 8, 2, 4, 2), ("y", "zl", "zh", "x", "c"))
    in_specs = (
        P(SECTION, None, DP, None),
        P(SECTION, None, DP, None),
        P(SECTION, None, None, None, None),
        P(SECTION, None, None, DP),
        P(SECTION, None, None, DP),
        P(SECTION, None, None, DP),
    )
    out_specs = (
        P(SECTION, None, None, DP),
        P(SECTION, None, None, DP),
        P(SECTION, None, None, DP),
        P(SECTION, None, None, None, None),
    )
    return jax.shard_map(body, mesh=fine, in_specs=in_specs, out_specs=out_specs, check_vma=False)
```

```python
import functools

import jax
import jax.numpy as jnp
from jax import lax
from jax.experimental import pallas as pl
from jax.experimental.pallas import tpu as pltpu
from jax.sharding import Mesh, PartitionSpec as P

D = 6144
FF = 24576
UNITS = 16
INV_WIDTH = 1.0 / D**0.5
INV_HIDDEN = 1.0 / FF**0.5

beta_one = 0.9
beta_two = 0.95
adam_eps = 1e-08
learn_rate = 0.05
decay_rate = 0.01
adam_steps = 10.0

SECTION = ("y", "zl")
DP = ("zh", "x", "c")
NEAR = ("x", "c")
FAR = ("y", "zl", "zh")

ANY = pl.BlockSpec(memory_space=pl.ANY)
HBM = pl.BlockSpec(memory_space=pltpu.HBM)
VMEM = pl.BlockSpec(memory_space=pltpu.VMEM)
BF16 = jnp.bfloat16
F32 = jnp.float32


def far_groups():
    groups = []
    for low in range(16):
        groups.append([w * 2 + zh for w in (low, 31 - low) for zh in range(2)])
    return groups


def wrap_route():
    route = []
    for left in range(7, 32, 8):
        right = (left + 1) % 32
        route += [(left, right), (right, left)]
    return route


def swap_route():
    return [(7, 23), (23, 7), (8, 24), (24, 8)]


def weights_route():
    route = []
    for w, v in wrap_route():
        for zh in range(2):
            route.append((w * 2 + zh, v * 2 + 1 - zh))
    return route


def shifted(block, distance):
    skipped = 7 if distance < 0 else 0
    route = [((i - distance) % 32, i) for i in range(32) if i % 8 != skipped]
    return lax.ppermute(block, SECTION, route)


def swap_cores(block):
    return lax.ppermute(block, "c", [(0, 1), (1, 0)])


def here(array):
    return pltpu.with_memory_space_constraint(array, pltpu.VMEM)


def call(kernel, outs, *args, specs=None, scratch=(), flops=0, moved=0, vmem=32):
    return pl.pallas_call(
        kernel,
        out_shape=[pltpu.VMEM(*out) if isinstance(out, tuple) else out for out in outs],
        in_specs=specs or [VMEM] * len(args),
        out_specs=[VMEM if isinstance(out, tuple) else ANY for out in outs],
        scratch_shapes=list(scratch),
        cost_estimate=pl.CostEstimate(flops=flops, bytes_accessed=moved, transcendentals=0),
        compiler_params=pltpu.CompilerParams(vmem_limit_bytes=vmem * 2**20),
    )(*args)


def gelu_exact(values):
    return 0.5 * values * (1.0 + lax.erf(values * 0.7071067811865476))


def gelu_slope(values):
    return (
        0.5 * (1.0 + lax.erf(values * 0.7071067811865476))
        + values * jnp.exp(-0.5 * values * values) * 0.3989422804014327
    )


def dot(a, b, ca, cb):
    return lax.dot_general(a, b, (((ca,), (cb,)), ((), ())), preferred_element_type=F32)


def take_weights_kernel(weights, w_out, sem):
    side = jnp.where(lax.axis_index("zl") == 7, 0, 1)
    pltpu.async_copy(weights.at[0, side, 1], w_out, sem).wait()


def take_grads_kernel(grads, down, up, sems):
    copies = [
        pltpu.make_async_copy(grads.at[0, 0], down, sems.at[0]),
        pltpu.make_async_copy(grads.at[0, 1], up, sems.at[1]),
    ]
    for copy in copies:
        copy.start()
    for copy in copies:
        copy.wait()


def forward_kernel(acts, weights, pre_act):
    for c in range(2):
        pre_act[c] = dot(weights[0, c, 0], acts[0, c], 1, 1) * INV_WIDTH


def wrap_kernel(w_out, down, up, pre_act, sent):
    left = lax.axis_index("zl") == 7

    @pl.when(left)
    def _():
        sent[:UNITS] = pre_act[0]
        sent[UNITS:] = dot(w_out[...], up[...], 1, 1) * INV_HIDDEN

    @pl.when(jnp.logical_not(left))
    def _():
        sent[:UNITS] = pre_act[1]
        sent[UNITS:] = dot(w_out[...], down[...], 1, 1) * INV_HIDDEN


def terms_kernel(
    from_after, from_before, wrapped, acts, weights, pre_act, down, up, keep, send, grad, factor
):
    zl = lax.axis_index("zl")
    first = lax.axis_index("c") == 0

    def product(lhs, rhs, scale, row):
        for block in range(8):
            x, zh = block % 4, block // 4
            even = dot(lhs, rhs(block * 768), 1, 0) * scale
            odd = dot(lhs, rhs(block * 768 + 384), 1, 0) * scale
            spot = (x, pl.ds(row, UNITS), pl.ds(zh * 384, 384))
            keep[spot] = jnp.where(first, even, odd)
            send[spot] = jnp.where(first, odd, even).astype(BF16)

    for c in range(2):
        wrap = zl == (7 if c == 0 else 0)
        upstream = from_after if c == 0 else from_before
        own = up if c == 0 else down

        @pl.when(wrap)
        def _():
            grad[...] = wrapped[UNITS:]
            factor[...] = wrapped[:UNITS]

        @pl.when(jnp.logical_not(wrap))
        def _():
            grad[...] = dot(weights[0, c, 1], upstream[...], 1, 1) * INV_HIDDEN
            factor[...] = pre_act[c]

        pre_grad = (grad[...] * gelu_slope(pre_act[c])).astype(BF16)
        activation = gelu_exact(factor[...]).astype(BF16)
        row = c * 2 * UNITS
        product(pre_grad, lambda at: acts[0, c, :, at : at + 384], INV_WIDTH, row)

        @pl.when(wrap)
        def _():
            product(activation, lambda at: own[:, at : at + 384], INV_HIDDEN, row + UNITS)

        @pl.when(jnp.logical_not(wrap))
        def _():
            product(activation, lambda at: upstream[:, at : at + 384], INV_HIDDEN, row + UNITS)


def merge_kernel(keep, arrived, out):
    out[...] = (keep[...] + arrived[...].astype(F32)).astype(BF16)


def near_kernel(arrived, total, swap):
    for row in range(4):
        rows = pl.ds(row * UNITS, UNITS)
        part = arrived[0, rows].astype(F32)
        for x in range(1, 4):
            part += arrived[x, rows].astype(F32)
        total[rows] = part.astype(BF16)
    side = jnp.where(lax.axis_index("zl") == 7, UNITS, 3 * UNITS)
    swap[...] = total[pl.ds(pl.multiple_of(side, UNITS), UNITS)]


def spread_kernel(total, swap, out):
    y, zl = lax.axis_index("y"), lax.axis_index("zl")
    upper = y >= 2
    for zh in range(2):
        columns = slice(zh * 384, zh * 384 + 384)
        for p in range(2):
            parts = []
            for c in range(2):
                part = total[(2 * c + p) * UNITS : (2 * c + p + 1) * UNITS, columns]
                if p == 1:
                    moved = (zl == (7 if c == 0 else 0)) & (y % 2 == c)
                    part = jnp.where(moved, swap[:, columns], part)
                parts.append(part)
            out[2 * p + zh, 0] = jnp.where(upper, parts[1], parts[0])
            out[2 * p + zh, 1] = jnp.where(upper, parts[0], parts[1])


def adam_kernel(arrived, master, moment, second, new_master, new_moment, new_second, shared):
    upper = lax.axis_index("y") >= 2
    sums = []
    for sec in range(2):
        part = arrived[0, sec].astype(F32)
        for i in range(1, 4):
            part += arrived[i, sec].astype(F32)
        sums.append(part)
    rounded = []
    for j in range(2):
        grad = jnp.where(upper, sums[1 - j], sums[j])
        moment_now = beta_one * moment[0, j] + (1.0 - beta_one) * grad
        second_now = beta_two * second[0, j] + (1.0 - beta_two) * grad * grad
        corrected = (
            moment_now
            / (1.0 - beta_one**adam_steps)
            / (jnp.sqrt(second_now / (1.0 - beta_two**adam_steps)) + adam_eps)
        )
        old = master[0, j]
        master_now = old - learn_rate * (corrected + decay_rate * old)
        new_master[0, j] = master_now
        new_moment[0, j] = moment_now
        new_second[0, j] = second_now
        rounded.append(master_now.astype(BF16))
    for sec in range(2):
        part = jnp.where(upper, rounded[1 - sec], rounded[sec])
        for i in range(4):
            shared[i, sec] = part


def finish_kernel(full, out, sem):
    upper = jnp.where(lax.axis_index("y") >= 2, 1, 0)
    copies = []
    for near in range(8):
        for zh in range(2):
            for sec in range(2):
                c = sec + upper - 2 * sec * upper
                at = (zh * 8 + near) * 384
                for p in range(2):
                    copies.append(
                        pltpu.make_async_copy(
                            full.at[near, 2 * p + zh, sec], out.at[0, c, p, :, pl.ds(at, 384)], sem
                        )
                    )
    for copy in copies:
        copy.start()
    for copy in copies:
        copy.wait()


def body(acts, grads_sent, replicas, master, moment, second):
    (w_out,) = call(
        take_weights_kernel,
        [((UNITS, D), BF16)],
        replicas, specs=[HBM], scratch=[pltpu.SemaphoreType.DMA], vmem=63,
    )
    w_out_moved = lax.ppermute(w_out, FAR, weights_route())
    down, up = call(
        take_grads_kernel,
        [((64, D), BF16), ((64, D), BF16)],
        grads_sent, specs=[HBM], scratch=[pltpu.SemaphoreType.DMA((2,))], vmem=60, flops=10**10,
    )
    from_after, from_before = shifted(down, -1), shifted(up, 1)
    acts, weights = here(acts), here(replicas)
    (pre_act,) = call(forward_kernel, [((2, UNITS, 64), F32)], acts, weights, flops=10**10)
    (sent,) = call(wrap_kernel, [((2 * UNITS, 64), F32)], here(w_out_moved), down, up, pre_act)
    wrapped = lax.ppermute(sent, SECTION, wrap_route())
    keep, send = call(
        terms_kernel,
        [((4, 64, 768), F32), ((4, 64, 768), BF16)],
        here(from_after), here(from_before), here(wrapped), acts, weights, pre_act, down, up,
        scratch=[pltpu.VMEM((UNITS, 64), F32), pltpu.VMEM((UNITS, 64), F32)],
    )
    arrived = swap_cores(send)
    (tiles,) = call(merge_kernel, [((4, 64, 768), BF16)], keep, here(arrived))
    near = lax.all_to_all(tiles, "x", 0, 0, tiled=True)
    total, swap = call(near_kernel, [((64, 768), BF16), ((UNITS, 768), BF16)], here(near))
    swap = lax.ppermute(swap, SECTION, swap_route())
    (spread,) = call(spread_kernel, [((4, 2, UNITS, 384), BF16)], total, here(swap))
    far = lax.all_to_all(spread, FAR, 0, 0, axis_index_groups=far_groups(), tiled=True)
    shard = ((1, 2, UNITS, 384), F32)
    new_master, new_moment, new_second, shared = call(
        adam_kernel,
        [shard, shard, shard, ((4, 2, UNITS, 384), BF16)],
        here(far), here(master), here(moment), here(second),
    )
    shared = lax.all_to_all(shared, FAR, 0, 0, axis_index_groups=far_groups(), tiled=True)
    full = lax.all_gather(shared, NEAR, axis=0, tiled=False)
    (new_replicas,) = call(
        finish_kernel,
        [jax.ShapeDtypeStruct((1, 2, 2, UNITS, D), BF16)],
        here(full), scratch=[pltpu.SemaphoreType.DMA],
    )
    return (new_master, new_moment, new_second, new_replicas)


def solution(mesh):
    fine = Mesh(mesh.devices.reshape(4, 8, 2, 4, 2), ("y", "zl", "zh", "x", "c"))
    in_specs = (
        P(SECTION, None, DP, None),
        P(SECTION, None, DP, None),
        P(SECTION, None, None, None, None),
        P(SECTION, None, None, DP),
        P(SECTION, None, None, DP),
        P(SECTION, None, None, DP),
    )
    out_specs = (
        P(SECTION, None, None, DP),
        P(SECTION, None, None, DP),
        P(SECTION, None, None, DP),
        P(SECTION, None, None, None, None),
    )
    return jax.shard_map(body, mesh=fine, in_specs=in_specs, out_specs=out_specs, check_vma=False)
```

```python
import functools

import jax
import jax.numpy as jnp
from jax import lax
from jax.experimental import pallas as pl
from jax.experimental.pallas import tpu as pltpu
from jax.sharding import Mesh, PartitionSpec as P

D = 6144
FF = 24576
UNITS = 16
INV_WIDTH = 1.0 / D**0.5
INV_HIDDEN = 1.0 / FF**0.5

beta_one = 0.9
beta_two = 0.95
adam_eps = 1e-08
learn_rate = 0.05
decay_rate = 0.01
adam_steps = 10.0

SECTION = ("y", "zl")
DP = ("zh", "x", "c")
NEAR = ("x", "c")
FAR = ("y", "zl", "zh")

ANY = pl.BlockSpec(memory_space=pl.ANY)
HBM = pl.BlockSpec(memory_space=pltpu.HBM)
VMEM = pl.BlockSpec(memory_space=pltpu.VMEM)
BF16 = jnp.bfloat16
F32 = jnp.float32


def far_groups():
    groups = []
    for low in range(16):
        groups.append([w * 2 + zh for w in (low, 31 - low) for zh in range(2)])
    return groups


def wrap_route():
    route = []
    for left in range(7, 32, 8):
        right = (left + 1) % 32
        route += [(left, right), (right, left)]
    return route


def swap_route():
    return [(7, 23), (23, 7), (8, 24), (24, 8)]


def weights_route():
    route = []
    for w, v in wrap_route():
        for zh in range(2):
            route.append((w * 2 + zh, v * 2 + 1 - zh))
    return route


def shifted(block, distance):
    skipped = 7 if distance < 0 else 0
    route = [((i - distance) % 32, i) for i in range(32) if i % 8 != skipped]
    return lax.ppermute(block, SECTION, route)


def swap_cores(block):
    return lax.ppermute(block, "c", [(0, 1), (1, 0)])


def here(array):
    return pltpu.with_memory_space_constraint(array, pltpu.VMEM)


def call(kernel, outs, *args, specs=None, scratch=(), flops=0, moved=0, vmem=32):
    return pl.pallas_call(
        kernel,
        out_shape=[pltpu.VMEM(*out) if isinstance(out, tuple) else out for out in outs],
        in_specs=specs or [VMEM] * len(args),
        out_specs=[VMEM if isinstance(out, tuple) else ANY for out in outs],
        scratch_shapes=list(scratch),
        cost_estimate=pl.CostEstimate(flops=flops, bytes_accessed=moved, transcendentals=0),
        compiler_params=pltpu.CompilerParams(vmem_limit_bytes=vmem * 2**20),
    )(*args)


def gelu_exact(values):
    return 0.5 * values * (1.0 + lax.erf(values * 0.7071067811865476))


def gelu_slope(values):
    return (
        0.5 * (1.0 + lax.erf(values * 0.7071067811865476))
        + values * jnp.exp(-0.5 * values * values) * 0.3989422804014327
    )


def dot(a, b, ca, cb):
    return lax.dot_general(a, b, (((ca,), (cb,)), ((), ())), preferred_element_type=F32)


def take_kernel(grads, weights, w_out, down, up, sems):
    side = jnp.where(lax.axis_index("zl") == 7, 0, 1)
    copies = [
        pltpu.make_async_copy(weights.at[0, side, 1], w_out, sems.at[0]),
        pltpu.make_async_copy(grads.at[0, 0], down, sems.at[1]),
        pltpu.make_async_copy(grads.at[0, 1], up, sems.at[2]),
    ]
    for copy in copies:
        copy.start()
    for copy in copies:
        copy.wait()


def forward_kernel(acts, weights, pre_act):
    for c in range(2):
        pre_act[c] = dot(weights[0, c, 0], acts[0, c], 1, 1) * INV_WIDTH


def wrap_kernel(w_out, down, up, pre_act, sent):
    left = lax.axis_index("zl") == 7

    @pl.when(left)
    def _():
        sent[:UNITS] = pre_act[0]
        sent[UNITS:] = dot(w_out[...], up[...], 1, 1) * INV_HIDDEN

    @pl.when(jnp.logical_not(left))
    def _():
        sent[:UNITS] = pre_act[1]
        sent[UNITS:] = dot(w_out[...], down[...], 1, 1) * INV_HIDDEN


def terms_kernel(
    from_after, from_before, wrapped, acts, weights, pre_act, down, up, keep, send, grad, factor
):
    zl = lax.axis_index("zl")
    first = lax.axis_index("c") == 0

    def product(lhs, rhs, scale, row):
        for block in range(8):
            x, zh = block % 4, block // 4
            even = dot(lhs, rhs(block * 768), 1, 0) * scale
            odd = dot(lhs, rhs(block * 768 + 384), 1, 0) * scale
            spot = (x, pl.ds(row, UNITS), pl.ds(zh * 384, 384))
            keep[spot] = jnp.where(first, even, odd)
            send[spot] = jnp.where(first, odd, even).astype(BF16)

    for c in range(2):
        wrap = zl == (7 if c == 0 else 0)
        upstream = from_after if c == 0 else from_before
        own = up if c == 0 else down

        @pl.when(wrap)
        def _():
            grad[...] = wrapped[UNITS:]
            factor[...] = wrapped[:UNITS]

        @pl.when(jnp.logical_not(wrap))
        def _():
            grad[...] = dot(weights[0, c, 1], upstream[...], 1, 1) * INV_HIDDEN
            factor[...] = pre_act[c]

        pre_grad = (grad[...] * gelu_slope(pre_act[c])).astype(BF16)
        activation = gelu_exact(factor[...]).astype(BF16)
        row = c * 2 * UNITS
        product(pre_grad, lambda at: acts[0, c, :, at : at + 384], INV_WIDTH, row)

        @pl.when(wrap)
        def _():
            product(activation, lambda at: own[:, at : at + 384], INV_HIDDEN, row + UNITS)

        @pl.when(jnp.logical_not(wrap))
        def _():
            product(activation, lambda at: upstream[:, at : at + 384], INV_HIDDEN, row + UNITS)


def merge_kernel(keep, arrived, out):
    out[...] = (keep[...] + arrived[...].astype(F32)).astype(BF16)


def near_kernel(arrived, total, swap):
    for row in range(4):
        rows = pl.ds(row * UNITS, UNITS)
        part = arrived[0, rows].astype(F32)
        for x in range(1, 4):
            part += arrived[x, rows].astype(F32)
        total[rows] = part.astype(BF16)
    side = jnp.where(lax.axis_index("zl") == 7, UNITS, 3 * UNITS)
    swap[...] = total[pl.ds(pl.multiple_of(side, UNITS), UNITS)]


def spread_kernel(total, swap, out):
    y, zl = lax.axis_index("y"), lax.axis_index("zl")
    upper = y >= 2
    for zh in range(2):
        columns = slice(zh * 384, zh * 384 + 384)
        for p in range(2):
            parts = []
            for c in range(2):
                part = total[(2 * c + p) * UNITS : (2 * c + p + 1) * UNITS, columns]
                if p == 1:
                    moved = (zl == (7 if c == 0 else 0)) & (y % 2 == c)
                    part = jnp.where(moved, swap[:, columns], part)
                parts.append(part)
            out[2 * p + zh, 0] = jnp.where(upper, parts[1], parts[0])
            out[2 * p + zh, 1] = jnp.where(upper, parts[0], parts[1])


def adam_kernel(arrived, master, moment, second, new_master, new_moment, new_second, shared):
    upper = lax.axis_index("y") >= 2
    sums = []
    for sec in range(2):
        part = arrived[0, sec].astype(F32)
        for i in range(1, 4):
            part += arrived[i, sec].astype(F32)
        sums.append(part)
    rounded = []
    for j in range(2):
        grad = jnp.where(upper, sums[1 - j], sums[j])
        moment_now = beta_one * moment[0, j] + (1.0 - beta_one) * grad
        second_now = beta_two * second[0, j] + (1.0 - beta_two) * grad * grad
        corrected = (
            moment_now
            / (1.0 - beta_one**adam_steps)
            / (jnp.sqrt(second_now / (1.0 - beta_two**adam_steps)) + adam_eps)
        )
        old = master[0, j]
        master_now = old - learn_rate * (corrected + decay_rate * old)
        new_master[0, j] = master_now
        new_moment[0, j] = moment_now
        new_second[0, j] = second_now
        rounded.append(master_now.astype(BF16))
    for sec in range(2):
        part = jnp.where(upper, rounded[1 - sec], rounded[sec])
        for i in range(4):
            shared[i, sec] = part


def finish_kernel(full, out, sem):
    upper = jnp.where(lax.axis_index("y") >= 2, 1, 0)
    copies = []
    for near in range(8):
        for zh in range(2):
            for sec in range(2):
                c = sec + upper - 2 * sec * upper
                at = (zh * 8 + near) * 384
                for p in range(2):
                    copies.append(
                        pltpu.make_async_copy(
                            full.at[near, 2 * p + zh, sec], out.at[0, c, p, :, pl.ds(at, 384)], sem
                        )
                    )
    for copy in copies:
        copy.start()
    for copy in copies:
        copy.wait()


def body(acts, grads_sent, replicas, master, moment, second):
    w_out, down, up = call(
        take_kernel,
        [((UNITS, D), BF16), ((64, D), BF16), ((64, D), BF16)],
        grads_sent, replicas, specs=[HBM, HBM],
        scratch=[pltpu.SemaphoreType.DMA((3,))], vmem=60,
    )
    w_out_moved = lax.ppermute(w_out, FAR, weights_route())
    from_after, from_before = shifted(down, -1), shifted(up, 1)
    acts, weights = here(acts), here(replicas)
    (pre_act,) = call(forward_kernel, [((2, UNITS, 64), F32)], acts, weights, flops=10**10)
    (sent,) = call(wrap_kernel, [((2 * UNITS, 64), F32)], here(w_out_moved), down, up, pre_act)
    wrapped = lax.ppermute(sent, SECTION, wrap_route())
    keep, send = call(
        terms_kernel,
        [((4, 64, 768), F32), ((4, 64, 768), BF16)],
        here(from_after), here(from_before), here(wrapped), acts, weights, pre_act, down, up,
        scratch=[pltpu.VMEM((UNITS, 64), F32), pltpu.VMEM((UNITS, 64), F32)],
    )
    arrived = swap_cores(send)
    (tiles,) = call(merge_kernel, [((4, 64, 768), BF16)], keep, here(arrived))
    near = lax.all_to_all(tiles, "x", 0, 0, tiled=True)
    total, swap = call(near_kernel, [((64, 768), BF16), ((UNITS, 768), BF16)], here(near))
    swap = lax.ppermute(swap, SECTION, swap_route())
    (spread,) = call(spread_kernel, [((4, 2, UNITS, 384), BF16)], total, here(swap))
    far = lax.all_to_all(spread, FAR, 0, 0, axis_index_groups=far_groups(), tiled=True)
    shard = ((1, 2, UNITS, 384), F32)
    new_master, new_moment, new_second, shared = call(
        adam_kernel,
        [shard, shard, shard, ((4, 2, UNITS, 384), BF16)],
        here(far), here(master), here(moment), here(second),
    )
    shared = lax.all_to_all(shared, FAR, 0, 0, axis_index_groups=far_groups(), tiled=True)
    full = lax.all_gather(shared, NEAR, axis=0, tiled=False)
    (new_replicas,) = call(
        finish_kernel,
        [jax.ShapeDtypeStruct((1, 2, 2, UNITS, D), BF16)],
        here(full), scratch=[pltpu.SemaphoreType.DMA],
    )
    return (new_master, new_moment, new_second, new_replicas)


def solution(mesh):
    fine = Mesh(mesh.devices.reshape(4, 8, 2, 4, 2), ("y", "zl", "zh", "x", "c"))
    in_specs = (
        P(SECTION, None, DP, None),
        P(SECTION, None, DP, None),
        P(SECTION, None, None, None, None),
        P(SECTION, None, None, DP),
        P(SECTION, None, None, DP),
        P(SECTION, None, None, DP),
    )
    out_specs = (
        P(SECTION, None, None, DP),
        P(SECTION, None, None, DP),
        P(SECTION, None, None, DP),
        P(SECTION, None, None, None, None),
    )
    return jax.shard_map(body, mesh=fine, in_specs=in_specs, out_specs=out_specs, check_vma=False)
```

```python
import functools

import jax
import jax.numpy as jnp
from jax import lax
from jax.experimental import pallas as pl
from jax.experimental.pallas import tpu as pltpu
from jax.sharding import Mesh, PartitionSpec as P

D = 6144
FF = 24576
UNITS = 16
INV_WIDTH = 1.0 / D**0.5
INV_HIDDEN = 1.0 / FF**0.5

beta_one = 0.9
beta_two = 0.95
adam_eps = 1e-08
learn_rate = 0.05
decay_rate = 0.01
adam_steps = 10.0

SECTION = ("y", "zl")
DP = ("zh", "x", "c")
NEAR = ("x", "c")
FAR = ("y", "zl", "zh")

ANY = pl.BlockSpec(memory_space=pl.ANY)
HBM = pl.BlockSpec(memory_space=pltpu.HBM)
VMEM = pl.BlockSpec(memory_space=pltpu.VMEM)
BF16 = jnp.bfloat16
F32 = jnp.float32


def far_groups():
    groups = []
    for low in range(16):
        groups.append([w * 2 + zh for w in (low, 31 - low) for zh in range(2)])
    return groups


def wrap_route():
    route = []
    for left in range(7, 32, 8):
        right = (left + 1) % 32
        route += [(left, right), (right, left)]
    return route


def swap_route():
    return [(7, 23), (23, 7), (8, 24), (24, 8)]


def weights_route():
    route = []
    for w, v in wrap_route():
        for zh in range(2):
            route.append((w * 2 + zh, v * 2 + 1 - zh))
    return route


def shifted(block, distance):
    skipped = 7 if distance < 0 else 0
    route = [((i - distance) % 32, i) for i in range(32) if i % 8 != skipped]
    return lax.ppermute(block, SECTION, route)


def swap_cores(block):
    return lax.ppermute(block, "c", [(0, 1), (1, 0)])


def here(array):
    return pltpu.with_memory_space_constraint(array, pltpu.VMEM)


def call(kernel, outs, *args, specs=None, scratch=(), flops=0, moved=0, vmem=32):
    return pl.pallas_call(
        kernel,
        out_shape=[pltpu.VMEM(*out) if isinstance(out, tuple) else out for out in outs],
        in_specs=specs or [VMEM] * len(args),
        out_specs=[VMEM if isinstance(out, tuple) else ANY for out in outs],
        scratch_shapes=list(scratch),
        cost_estimate=pl.CostEstimate(flops=flops, bytes_accessed=moved, transcendentals=0),
        compiler_params=pltpu.CompilerParams(vmem_limit_bytes=vmem * 2**20),
    )(*args)


def gelu_exact(values):
    return 0.5 * values * (1.0 + lax.erf(values * 0.7071067811865476))


def gelu_slope(values):
    return (
        0.5 * (1.0 + lax.erf(values * 0.7071067811865476))
        + values * jnp.exp(-0.5 * values * values) * 0.3989422804014327
    )


def dot(a, b, ca, cb):
    return lax.dot_general(a, b, (((ca,), (cb,)), ((), ())), preferred_element_type=F32)


def take_kernel(grads, weights, w_out, down, up, sems):
    side = jnp.where(lax.axis_index("zl") == 7, 0, 1)
    copies = [
        pltpu.make_async_copy(weights.at[0, side, 1], w_out, sems.at[0]),
        pltpu.make_async_copy(grads.at[0, 0], down, sems.at[1]),
        pltpu.make_async_copy(grads.at[0, 1], up, sems.at[2]),
    ]
    for copy in copies:
        copy.start()
    for copy in copies:
        copy.wait()


def after_kernel(_, value, out):
    del value, out


def after(first, value, flops):
    return pl.pallas_call(
        after_kernel,
        out_shape=pltpu.VMEM(value.shape, value.dtype),
        in_specs=[VMEM, VMEM],
        out_specs=VMEM,
        input_output_aliases={1: 0},
        cost_estimate=pl.CostEstimate(flops=flops, bytes_accessed=0, transcendentals=0),
    )(here(first), here(value))


def forward_kernel(acts, weights, pre_act):
    for c in range(2):
        pre_act[c] = dot(weights[0, c, 0], acts[0, c], 1, 1) * INV_WIDTH


def wrap_kernel(w_out, down, up, pre_act, sent):
    left = lax.axis_index("zl") == 7

    @pl.when(left)
    def _():
        sent[:UNITS] = pre_act[0]
        sent[UNITS:] = dot(w_out[...], up[...], 1, 1) * INV_HIDDEN

    @pl.when(jnp.logical_not(left))
    def _():
        sent[:UNITS] = pre_act[1]
        sent[UNITS:] = dot(w_out[...], down[...], 1, 1) * INV_HIDDEN


def terms_kernel(
    from_after, from_before, wrapped, acts, weights, pre_act, down, up, keep, send, grad, factor
):
    zl = lax.axis_index("zl")
    first = lax.axis_index("c") == 0

    def product(lhs, rhs, scale, row):
        for block in range(8):
            x, zh = block % 4, block // 4
            even = dot(lhs, rhs(block * 768), 1, 0) * scale
            odd = dot(lhs, rhs(block * 768 + 384), 1, 0) * scale
            spot = (x, pl.ds(row, UNITS), pl.ds(zh * 384, 384))
            keep[spot] = jnp.where(first, even, odd)
            send[spot] = jnp.where(first, odd, even).astype(BF16)

    for c in range(2):
        wrap = zl == (7 if c == 0 else 0)
        upstream = from_after if c == 0 else from_before
        own = up if c == 0 else down

        @pl.when(wrap)
        def _():
            grad[...] = wrapped[UNITS:]
            factor[...] = wrapped[:UNITS]

        @pl.when(jnp.logical_not(wrap))
        def _():
            grad[...] = dot(weights[0, c, 1], upstream[...], 1, 1) * INV_HIDDEN
            factor[...] = pre_act[c]

        pre_grad = (grad[...] * gelu_slope(pre_act[c])).astype(BF16)
        activation = gelu_exact(factor[...]).astype(BF16)
        row = c * 2 * UNITS
        product(pre_grad, lambda at: acts[0, c, :, at : at + 384], INV_WIDTH, row)

        @pl.when(wrap)
        def _():
            product(activation, lambda at: own[:, at : at + 384], INV_HIDDEN, row + UNITS)

        @pl.when(jnp.logical_not(wrap))
        def _():
            product(activation, lambda at: upstream[:, at : at + 384], INV_HIDDEN, row + UNITS)


def merge_kernel(keep, arrived, out):
    out[...] = (keep[...] + arrived[...].astype(F32)).astype(BF16)


def near_kernel(arrived, total, swap):
    for row in range(4):
        rows = pl.ds(row * UNITS, UNITS)
        part = arrived[0, rows].astype(F32)
        for x in range(1, 4):
            part += arrived[x, rows].astype(F32)
        total[rows] = part.astype(BF16)
    side = jnp.where(lax.axis_index("zl") == 7, UNITS, 3 * UNITS)
    swap[...] = total[pl.ds(pl.multiple_of(side, UNITS), UNITS)]


def spread_kernel(total, swap, out):
    y, zl = lax.axis_index("y"), lax.axis_index("zl")
    upper = y >= 2
    for zh in range(2):
        columns = slice(zh * 384, zh * 384 + 384)
        for p in range(2):
            parts = []
            for c in range(2):
                part = total[(2 * c + p) * UNITS : (2 * c + p + 1) * UNITS, columns]
                if p == 1:
                    moved = (zl == (7 if c == 0 else 0)) & (y % 2 == c)
                    part = jnp.where(moved, swap[:, columns], part)
                parts.append(part)
            out[2 * p + zh, 0] = jnp.where(upper, parts[1], parts[0])
            out[2 * p + zh, 1] = jnp.where(upper, parts[0], parts[1])


def adam_kernel(arrived, master, moment, second, new_master, new_moment, new_second, shared):
    upper = lax.axis_index("y") >= 2
    sums = []
    for sec in range(2):
        part = arrived[0, sec].astype(F32)
        for i in range(1, 4):
            part += arrived[i, sec].astype(F32)
        sums.append(part)
    rounded = []
    for j in range(2):
        grad = jnp.where(upper, sums[1 - j], sums[j])
        moment_now = beta_one * moment[0, j] + (1.0 - beta_one) * grad
        second_now = beta_two * second[0, j] + (1.0 - beta_two) * grad * grad
        corrected = (
            moment_now
            / (1.0 - beta_one**adam_steps)
            / (jnp.sqrt(second_now / (1.0 - beta_two**adam_steps)) + adam_eps)
        )
        old = master[0, j]
        master_now = old - learn_rate * (corrected + decay_rate * old)
        new_master[0, j] = master_now
        new_moment[0, j] = moment_now
        new_second[0, j] = second_now
        rounded.append(master_now.astype(BF16))
    for sec in range(2):
        part = jnp.where(upper, rounded[1 - sec], rounded[sec])
        for i in range(4):
            shared[i, sec] = part


def finish_kernel(full, out, sem):
    upper = jnp.where(lax.axis_index("y") >= 2, 1, 0)
    copies = []
    for near in range(8):
        for zh in range(2):
            for sec in range(2):
                c = sec + upper - 2 * sec * upper
                at = (zh * 8 + near) * 384
                for p in range(2):
                    copies.append(
                        pltpu.make_async_copy(
                            full.at[near, 2 * p + zh, sec], out.at[0, c, p, :, pl.ds(at, 384)], sem
                        )
                    )
    for copy in copies:
        copy.start()
    for copy in copies:
        copy.wait()


def body(acts, grads_sent, replicas, master, moment, second):
    w_out, down, up = call(
        take_kernel,
        [((UNITS, D), BF16), ((64, D), BF16), ((64, D), BF16)],
        grads_sent, replicas, specs=[HBM, HBM],
        scratch=[pltpu.SemaphoreType.DMA((3,))], vmem=60,
    )
    from_before = shifted(up, 1)
    w_out = after(up, w_out, 10**10)
    w_out_moved = lax.ppermute(w_out, FAR, weights_route())
    down = after(w_out, down, 10**10)
    from_after = shifted(down, -1)
    acts, weights = here(acts), here(replicas)
    (pre_act,) = call(forward_kernel, [((2, UNITS, 64), F32)], acts, weights, flops=10**10)
    (sent,) = call(wrap_kernel, [((2 * UNITS, 64), F32)], here(w_out_moved), down, up, pre_act)
    wrapped = lax.ppermute(sent, SECTION, wrap_route())
    keep, send = call(
        terms_kernel,
        [((4, 64, 768), F32), ((4, 64, 768), BF16)],
        here(from_after), here(from_before), here(wrapped), acts, weights, pre_act, down, up,
        scratch=[pltpu.VMEM((UNITS, 64), F32), pltpu.VMEM((UNITS, 64), F32)],
    )
    arrived = swap_cores(send)
    (tiles,) = call(merge_kernel, [((4, 64, 768), BF16)], keep, here(arrived))
    near = lax.all_to_all(tiles, "x", 0, 0, tiled=True)
    total, swap = call(near_kernel, [((64, 768), BF16), ((UNITS, 768), BF16)], here(near))
    swap = lax.ppermute(swap, SECTION, swap_route())
    (spread,) = call(spread_kernel, [((4, 2, UNITS, 384), BF16)], total, here(swap))
    far = lax.all_to_all(spread, FAR, 0, 0, axis_index_groups=far_groups(), tiled=True)
    shard = ((1, 2, UNITS, 384), F32)
    new_master, new_moment, new_second, shared = call(
        adam_kernel,
        [shard, shard, shard, ((4, 2, UNITS, 384), BF16)],
        here(far), here(master), here(moment), here(second),
    )
    shared = lax.all_to_all(shared, FAR, 0, 0, axis_index_groups=far_groups(), tiled=True)
    full = lax.all_gather(shared, NEAR, axis=0, tiled=False)
    (new_replicas,) = call(
        finish_kernel,
        [jax.ShapeDtypeStruct((1, 2, 2, UNITS, D), BF16)],
        here(full), scratch=[pltpu.SemaphoreType.DMA],
    )
    return (new_master, new_moment, new_second, new_replicas)


def solution(mesh):
    fine = Mesh(mesh.devices.reshape(4, 8, 2, 4, 2), ("y", "zl", "zh", "x", "c"))
    in_specs = (
        P(SECTION, None, DP, None),
        P(SECTION, None, DP, None),
        P(SECTION, None, None, None, None),
        P(SECTION, None, None, DP),
        P(SECTION, None, None, DP),
        P(SECTION, None, None, DP),
    )
    out_specs = (
        P(SECTION, None, None, DP),
        P(SECTION, None, None, DP),
        P(SECTION, None, None, DP),
        P(SECTION, None, None, None, None),
    )
    return jax.shard_map(body, mesh=fine, in_specs=in_specs, out_specs=out_specs, check_vma=False)
```

```python
import functools

import jax
import jax.numpy as jnp
from jax import lax
from jax.experimental import pallas as pl
from jax.experimental.pallas import tpu as pltpu
from jax.sharding import Mesh, PartitionSpec as P

D = 6144
FF = 24576
UNITS = 16
INV_WIDTH = 1.0 / D**0.5
INV_HIDDEN = 1.0 / FF**0.5

beta_one = 0.9
beta_two = 0.95
adam_eps = 1e-08
learn_rate = 0.05
decay_rate = 0.01
adam_steps = 10.0

SECTION = ("y", "zl")
DP = ("zh", "x", "c")
NEAR = ("x", "c")
FAR = ("y", "zl", "zh")

ANY = pl.BlockSpec(memory_space=pl.ANY)
HBM = pl.BlockSpec(memory_space=pltpu.HBM)
VMEM = pl.BlockSpec(memory_space=pltpu.VMEM)
BF16 = jnp.bfloat16
F32 = jnp.float32


def far_groups():
    groups = []
    for low in range(16):
        groups.append([w * 2 + zh for w in (low, 31 - low) for zh in range(2)])
    return groups


def wrap_route():
    route = []
    for left in range(7, 32, 8):
        right = (left + 1) % 32
        route += [(left, right), (right, left)]
    return route


def swap_route():
    return [(7, 23), (23, 7), (8, 24), (24, 8)]


def weights_route():
    route = []
    for w, v in wrap_route():
        for zh in range(2):
            route.append((w * 2 + zh, v * 2 + 1 - zh))
    return route


def shifted(block, distance, senders):
    route = [(w, (w + distance) % 32) for w in range(32) if w % 8 in senders]
    return lax.ppermute(block, SECTION, route)


def swap_cores(block):
    return lax.ppermute(block, "c", [(0, 1), (1, 0)])


def here(array):
    return pltpu.with_memory_space_constraint(array, pltpu.VMEM)


def call(kernel, outs, *args, specs=None, scratch=(), flops=0, moved=0, vmem=32):
    return pl.pallas_call(
        kernel,
        out_shape=[pltpu.VMEM(*out) if isinstance(out, tuple) else out for out in outs],
        in_specs=specs or [VMEM] * len(args),
        out_specs=[VMEM if isinstance(out, tuple) else ANY for out in outs],
        scratch_shapes=list(scratch),
        cost_estimate=pl.CostEstimate(flops=flops, bytes_accessed=moved, transcendentals=0),
        compiler_params=pltpu.CompilerParams(vmem_limit_bytes=vmem * 2**20),
    )(*args)


def gelu_exact(values):
    return 0.5 * values * (1.0 + lax.erf(values * 0.7071067811865476))


def gelu_slope(values):
    return (
        0.5 * (1.0 + lax.erf(values * 0.7071067811865476))
        + values * jnp.exp(-0.5 * values * values) * 0.3989422804014327
    )


def dot(a, b, ca, cb):
    return lax.dot_general(a, b, (((ca,), (cb,)), ((), ())), preferred_element_type=F32)


def joined(*parts):
    return jnp.concatenate([part[...] for part in parts], axis=0)


def columns(parts, at):
    return joined(*[part.at[:, at : at + 384] for part in parts])


def take_kernel(grads, weights, w_out, down, down_a, down_b, up, sems):
    side = jnp.where(lax.axis_index("zl") == 7, 0, 1)
    copies = [
        pltpu.make_async_copy(weights.at[0, side, 1], w_out, sems.at[0]),
        pltpu.make_async_copy(grads.at[0, 1], up, sems.at[1]),
        pltpu.make_async_copy(grads.at[0, 0], down, sems.at[2]),
        pltpu.make_async_copy(grads.at[0, 0, :32], down_a, sems.at[3]),
        pltpu.make_async_copy(grads.at[0, 0, 32:], down_b, sems.at[4]),
    ]
    for copy in copies:
        copy.start()
    for copy in copies:
        copy.wait()


def after_kernel(_, value, out):
    del value, out


def after(first, value, flops):
    return pl.pallas_call(
        after_kernel,
        out_shape=pltpu.VMEM(value.shape, value.dtype),
        in_specs=[VMEM, VMEM],
        out_specs=VMEM,
        input_output_aliases={1: 0},
        cost_estimate=pl.CostEstimate(flops=flops, bytes_accessed=0, transcendentals=0),
        compiler_params=pltpu.CompilerParams(vmem_limit_bytes=2 * 2**20),
    )(here(first), here(value))


def forward_kernel(acts, weights, pre_act):
    for c in range(2):
        pre_act[c] = dot(weights[0, c, 0], acts[0, c], 1, 1) * INV_WIDTH


def wrap_kernel(w_out, down, up, pre_act, sent):
    left = lax.axis_index("zl") == 7

    @pl.when(left)
    def _():
        sent[:UNITS] = pre_act[0]
        sent[UNITS:] = dot(w_out[...], up[...], 1, 1) * INV_HIDDEN

    @pl.when(jnp.logical_not(left))
    def _():
        sent[:UNITS] = pre_act[1]
        sent[UNITS:] = dot(w_out[...], down[...], 1, 1) * INV_HIDDEN


def terms_kernel(
    from_after, after_a, after_b, from_before, wrapped, acts, weights, pre_act, down, up,
    keep, send, grad, factor,
):
    zl = lax.axis_index("zl")
    first = lax.axis_index("c") == 0

    def product(lhs, rhs, scale, row):
        for block in range(8):
            x, zh = block % 4, block // 4
            even = dot(lhs, columns(rhs, block * 768), 1, 0) * scale
            odd = dot(lhs, columns(rhs, block * 768 + 384), 1, 0) * scale
            spot = (x, pl.ds(row, UNITS), pl.ds(zh * 384, 384))
            keep[spot] = jnp.where(first, even, odd)
            send[spot] = jnp.where(first, odd, even).astype(BF16)

    for c in range(2):
        wrap = zl == (7 if c == 0 else 0)
        if c == 0:
            own = up
            beside = zl == 6
            sources = [
                (jnp.logical_not(wrap | beside), (from_after,)),
                (beside, (after_a, after_b)),
            ]
        else:
            own = down
            sources = [(jnp.logical_not(wrap), (from_before,))]

        @pl.when(wrap)
        def _():
            grad[...] = wrapped[UNITS:]
            factor[...] = wrapped[:UNITS]

        for chosen, upstream in sources:

            @pl.when(chosen)
            def _():
                grad[...] = dot(weights[0, c, 1], joined(*upstream), 1, 1) * INV_HIDDEN
                factor[...] = pre_act[c]

        pre_grad = (grad[...] * gelu_slope(pre_act[c])).astype(BF16)
        activation = gelu_exact(factor[...]).astype(BF16)
        row = c * 2 * UNITS
        product(pre_grad, (acts.at[0, c],), INV_WIDTH, row)
        for chosen, upstream in [(wrap, (own,))] + sources:

            @pl.when(chosen)
            def _():
                product(activation, upstream, INV_HIDDEN, row + UNITS)


def merge_kernel(keep, arrived, out):
    out[...] = (keep[...] + arrived[...].astype(F32)).astype(BF16)


def near_kernel(arrived, total, swap):
    for row in range(4):
        rows = pl.ds(row * UNITS, UNITS)
        part = arrived[0, rows].astype(F32)
        for x in range(1, 4):
            part += arrived[x, rows].astype(F32)
        total[rows] = part.astype(BF16)
    side = jnp.where(lax.axis_index("zl") == 7, UNITS, 3 * UNITS)
    swap[...] = total[pl.ds(pl.multiple_of(side, UNITS), UNITS)]


def spread_kernel(total, swap, out):
    y, zl = lax.axis_index("y"), lax.axis_index("zl")
    upper = y >= 2
    for zh in range(2):
        columns = slice(zh * 384, zh * 384 + 384)
        for p in range(2):
            parts = []
            for c in range(2):
                part = total[(2 * c + p) * UNITS : (2 * c + p + 1) * UNITS, columns]
                if p == 1:
                    moved = (zl == (7 if c == 0 else 0)) & (y % 2 == c)
                    part = jnp.where(moved, swap[:, columns], part)
                parts.append(part)
            out[2 * p + zh, 0] = jnp.where(upper, parts[1], parts[0])
            out[2 * p + zh, 1] = jnp.where(upper, parts[0], parts[1])


def adam_kernel(arrived, master, moment, second, new_master, new_moment, new_second, shared):
    upper = lax.axis_index("y") >= 2
    sums = []
    for sec in range(2):
        part = arrived[0, sec].astype(F32)
        for i in range(1, 4):
            part += arrived[i, sec].astype(F32)
        sums.append(part)
    rounded = []
    for j in range(2):
        grad = jnp.where(upper, sums[1 - j], sums[j])
        moment_now = beta_one * moment[0, j] + (1.0 - beta_one) * grad
        second_now = beta_two * second[0, j] + (1.0 - beta_two) * grad * grad
        corrected = (
            moment_now
            / (1.0 - beta_one**adam_steps)
            / (jnp.sqrt(second_now / (1.0 - beta_two**adam_steps)) + adam_eps)
        )
        old = master[0, j]
        master_now = old - learn_rate * (corrected + decay_rate * old)
        new_master[0, j] = master_now
        new_moment[0, j] = moment_now
        new_second[0, j] = second_now
        rounded.append(master_now.astype(BF16))
    for sec in range(2):
        part = jnp.where(upper, rounded[1 - sec], rounded[sec])
        for i in range(4):
            shared[i, sec] = part


def finish_kernel(full, out, sem):
    upper = jnp.where(lax.axis_index("y") >= 2, 1, 0)
    copies = []
    for near in range(8):
        for zh in range(2):
            for sec in range(2):
                c = sec + upper - 2 * sec * upper
                at = (zh * 8 + near) * 384
                for p in range(2):
                    copies.append(
                        pltpu.make_async_copy(
                            full.at[near, 2 * p + zh, sec], out.at[0, c, p, :, pl.ds(at, 384)], sem
                        )
                    )
    for copy in copies:
        copy.start()
    for copy in copies:
        copy.wait()


def body(acts, grads_sent, replicas, master, moment, second):
    half = ((32, D), BF16)
    w_out, down, down_a, down_b, up = call(
        take_kernel,
        [((UNITS, D), BF16), ((64, D), BF16), half, half, ((64, D), BF16)],
        grads_sent, replicas, specs=[HBM, HBM],
        scratch=[pltpu.SemaphoreType.DMA((5,))], vmem=58,
    )
    from_before = shifted(up, 1, range(7))
    down = after(up, down, 10**10)
    from_after = shifted(down, -1, range(1, 7))
    w_out = after(down, w_out, 10**10)
    w_out_moved = lax.ppermute(w_out, FAR, weights_route())
    down_a = after(w_out, down_a, 10**10)
    after_a = shifted(down_a, -1, (7,))
    acts, weights = here(acts), here(replicas)
    (pre_act,) = call(forward_kernel, [((2, UNITS, 64), F32)], acts, weights, flops=10**10)
    (sent,) = call(
        wrap_kernel, [((2 * UNITS, 64), F32)], here(w_out_moved), down, up, pre_act
    )
    wrapped = lax.ppermute(sent, SECTION, wrap_route())
    down_b = after(sent, down_b, 10**10)
    after_b = shifted(down_b, -1, (7,))
    pre_act = after(down_b, pre_act, 10**10)
    keep, send = call(
        terms_kernel,
        [((4, 64, 768), F32), ((4, 64, 768), BF16)],
        here(from_after), here(after_a), here(after_b), here(from_before), here(wrapped),
        acts, weights, pre_act, down, up,
        scratch=[pltpu.VMEM((UNITS, 64), F32), pltpu.VMEM((UNITS, 64), F32)],
    )
    arrived = swap_cores(send)
    (tiles,) = call(merge_kernel, [((4, 64, 768), BF16)], keep, here(arrived))
    near = lax.all_to_all(tiles, "x", 0, 0, tiled=True)
    total, swap = call(near_kernel, [((64, 768), BF16), ((UNITS, 768), BF16)], here(near))
    swap = lax.ppermute(swap, SECTION, swap_route())
    (spread,) = call(spread_kernel, [((4, 2, UNITS, 384), BF16)], total, here(swap))
    far = lax.all_to_all(spread, FAR, 0, 0, axis_index_groups=far_groups(), tiled=True)
    shard = ((1, 2, UNITS, 384), F32)
    new_master, new_moment, new_second, shared = call(
        adam_kernel,
        [shard, shard, shard, ((4, 2, UNITS, 384), BF16)],
        here(far), here(master), here(moment), here(second),
    )
    shared = lax.all_to_all(shared, FAR, 0, 0, axis_index_groups=far_groups(), tiled=True)
    full = lax.all_gather(shared, NEAR, axis=0, tiled=False)
    (new_replicas,) = call(
        finish_kernel,
        [jax.ShapeDtypeStruct((1, 2, 2, UNITS, D), BF16)],
        here(full), scratch=[pltpu.SemaphoreType.DMA],
    )
    return (new_master, new_moment, new_second, new_replicas)


def solution(mesh):
    fine = Mesh(mesh.devices.reshape(4, 8, 2, 4, 2), ("y", "zl", "zh", "x", "c"))
    in_specs = (
        P(SECTION, None, DP, None),
        P(SECTION, None, DP, None),
        P(SECTION, None, None, None, None),
        P(SECTION, None, None, DP),
        P(SECTION, None, None, DP),
        P(SECTION, None, None, DP),
    )
    out_specs = (
        P(SECTION, None, None, DP),
        P(SECTION, None, None, DP),
        P(SECTION, None, None, DP),
        P(SECTION, None, None, None, None),
    )
    return jax.shard_map(body, mesh=fine, in_specs=in_specs, out_specs=out_specs, check_vma=False)
```

```python
import functools

import jax
import jax.numpy as jnp
from jax import lax
from jax.experimental import pallas as pl
from jax.experimental.pallas import tpu as pltpu
from jax.sharding import Mesh, PartitionSpec as P

D = 6144
FF = 24576
UNITS = 16
INV_WIDTH = 1.0 / D**0.5
INV_HIDDEN = 1.0 / FF**0.5

beta_one = 0.9
beta_two = 0.95
adam_eps = 1e-08
learn_rate = 0.05
decay_rate = 0.01
adam_steps = 10.0

SECTION = ("y", "zl")
DP = ("zh", "x", "c")
NEAR = ("x", "c")
FAR = ("y", "zl", "zh")

ANY = pl.BlockSpec(memory_space=pl.ANY)
HBM = pl.BlockSpec(memory_space=pltpu.HBM)
VMEM = pl.BlockSpec(memory_space=pltpu.VMEM)
BF16 = jnp.bfloat16
F32 = jnp.float32


def far_groups():
    groups = []
    for low in range(16):
        groups.append([w * 2 + zh for w in (low, 31 - low) for zh in range(2)])
    return groups


def wrap_route():
    route = []
    for left in range(7, 32, 8):
        right = (left + 1) % 32
        route += [(left, right), (right, left)]
    return route


def swap_route():
    return [(7, 23), (23, 7), (8, 24), (24, 8)]


def weights_route():
    route = []
    for w, v in wrap_route():
        for zh in range(2):
            route.append((w * 2 + zh, v * 2 + 1 - zh))
    return route


def shifted(block, distance, senders):
    route = [(w, (w + distance) % 32) for w in range(32) if w % 8 in senders]
    return lax.ppermute(block, SECTION, route)


def swap_cores(block):
    return lax.ppermute(block, "c", [(0, 1), (1, 0)])


def here(array):
    return pltpu.with_memory_space_constraint(array, pltpu.VMEM)


def call(kernel, outs, *args, specs=None, scratch=(), flops=0, moved=0, vmem=32):
    return pl.pallas_call(
        kernel,
        out_shape=[pltpu.VMEM(*out) if isinstance(out, tuple) else out for out in outs],
        in_specs=specs or [VMEM] * len(args),
        out_specs=[VMEM if isinstance(out, tuple) else ANY for out in outs],
        scratch_shapes=list(scratch),
        cost_estimate=pl.CostEstimate(flops=flops, bytes_accessed=moved, transcendentals=0),
        compiler_params=pltpu.CompilerParams(vmem_limit_bytes=vmem * 2**20),
    )(*args)


def gelu_exact(values):
    return 0.5 * values * (1.0 + lax.erf(values * 0.7071067811865476))


def gelu_slope(values):
    return (
        0.5 * (1.0 + lax.erf(values * 0.7071067811865476))
        + values * jnp.exp(-0.5 * values * values) * 0.3989422804014327
    )


def dot(a, b, ca, cb):
    return lax.dot_general(a, b, (((ca,), (cb,)), ((), ())), preferred_element_type=F32)


def joined(*parts):
    return jnp.concatenate([part[...] for part in parts], axis=0)


def columns(parts, at):
    return joined(*[part.at[:, at : at + 384] for part in parts])


def take_kernel(grads, weights, w_out, down, down_a, down_b, up, sems):
    side = jnp.where(lax.axis_index("zl") == 7, 0, 1)
    copies = [
        pltpu.make_async_copy(weights.at[0, side, 1], w_out, sems.at[0]),
        pltpu.make_async_copy(grads.at[0, 1], up, sems.at[1]),
        pltpu.make_async_copy(grads.at[0, 0], down, sems.at[2]),
        pltpu.make_async_copy(grads.at[0, 0, :48], down_a, sems.at[3]),
        pltpu.make_async_copy(grads.at[0, 0, 48:], down_b, sems.at[4]),
    ]
    for copy in copies:
        copy.start()
    for copy in copies:
        copy.wait()


def after_kernel(_, value, out):
    del value, out


def after(first, value, flops):
    return pl.pallas_call(
        after_kernel,
        out_shape=pltpu.VMEM(value.shape, value.dtype),
        in_specs=[VMEM, VMEM],
        out_specs=VMEM,
        input_output_aliases={1: 0},
        cost_estimate=pl.CostEstimate(flops=flops, bytes_accessed=0, transcendentals=0),
        compiler_params=pltpu.CompilerParams(vmem_limit_bytes=2 * 2**20),
    )(here(first), here(value))


def forward_kernel(acts, weights, pre_act):
    for c in range(2):
        pre_act[c] = dot(weights[0, c, 0], acts[0, c], 1, 1) * INV_WIDTH


def wrap_kernel(w_out, down, up, pre_act, sent):
    left = lax.axis_index("zl") == 7

    @pl.when(left)
    def _():
        sent[:UNITS] = pre_act[0]
        sent[UNITS:] = dot(w_out[...], up[...], 1, 1) * INV_HIDDEN

    @pl.when(jnp.logical_not(left))
    def _():
        sent[:UNITS] = pre_act[1]
        sent[UNITS:] = dot(w_out[...], down[...], 1, 1) * INV_HIDDEN


def terms_kernel(
    from_after, after_a, after_b, from_before, wrapped, acts, weights, pre_act, down, up,
    keep, send, grad, factor,
):
    zl = lax.axis_index("zl")
    first = lax.axis_index("c") == 0

    def product(lhs, rhs, scale, row):
        for block in range(8):
            x, zh = block % 4, block // 4
            even = dot(lhs, columns(rhs, block * 768), 1, 0) * scale
            odd = dot(lhs, columns(rhs, block * 768 + 384), 1, 0) * scale
            spot = (x, pl.ds(row, UNITS), pl.ds(zh * 384, 384))
            keep[spot] = jnp.where(first, even, odd)
            send[spot] = jnp.where(first, odd, even).astype(BF16)

    for c in range(2):
        wrap = zl == (7 if c == 0 else 0)
        if c == 0:
            own = up
            beside = zl == 6
            sources = [
                (jnp.logical_not(wrap | beside), (from_after,)),
                (beside, (after_a, after_b)),
            ]
        else:
            own = down
            sources = [(jnp.logical_not(wrap), (from_before,))]

        @pl.when(wrap)
        def _():
            grad[...] = wrapped[UNITS:]
            factor[...] = wrapped[:UNITS]

        for chosen, upstream in sources:

            @pl.when(chosen)
            def _():
                grad[...] = dot(weights[0, c, 1], joined(*upstream), 1, 1) * INV_HIDDEN
                factor[...] = pre_act[c]

        pre_grad = (grad[...] * gelu_slope(pre_act[c])).astype(BF16)
        activation = gelu_exact(factor[...]).astype(BF16)
        row = c * 2 * UNITS
        product(pre_grad, (acts.at[0, c],), INV_WIDTH, row)
        for chosen, upstream in [(wrap, (own,))] + sources:

            @pl.when(chosen)
            def _():
                product(activation, upstream, INV_HIDDEN, row + UNITS)


def merge_kernel(keep, arrived, out):
    out[...] = (keep[...] + arrived[...].astype(F32)).astype(BF16)


def near_kernel(arrived, total, swap):
    for row in range(4):
        rows = pl.ds(row * UNITS, UNITS)
        part = arrived[0, rows].astype(F32)
        for x in range(1, 4):
            part += arrived[x, rows].astype(F32)
        total[rows] = part.astype(BF16)
    side = jnp.where(lax.axis_index("zl") == 7, UNITS, 3 * UNITS)
    swap[...] = total[pl.ds(pl.multiple_of(side, UNITS), UNITS)]


def spread_kernel(total, swap, out):
    y, zl = lax.axis_index("y"), lax.axis_index("zl")
    upper = y >= 2
    for zh in range(2):
        columns = slice(zh * 384, zh * 384 + 384)
        for p in range(2):
            parts = []
            for c in range(2):
                part = total[(2 * c + p) * UNITS : (2 * c + p + 1) * UNITS, columns]
                if p == 1:
                    moved = (zl == (7 if c == 0 else 0)) & (y % 2 == c)
                    part = jnp.where(moved, swap[:, columns], part)
                parts.append(part)
            out[2 * p + zh, 0] = jnp.where(upper, parts[1], parts[0])
            out[2 * p + zh, 1] = jnp.where(upper, parts[0], parts[1])


def adam_kernel(arrived, master, moment, second, new_master, new_moment, new_second, shared):
    upper = lax.axis_index("y") >= 2
    sums = []
    for sec in range(2):
        part = arrived[0, sec].astype(F32)
        for i in range(1, 4):
            part += arrived[i, sec].astype(F32)
        sums.append(part)
    rounded = []
    for j in range(2):
        grad = jnp.where(upper, sums[1 - j], sums[j])
        moment_now = beta_one * moment[0, j] + (1.0 - beta_one) * grad
        second_now = beta_two * second[0, j] + (1.0 - beta_two) * grad * grad
        corrected = (
            moment_now
            / (1.0 - beta_one**adam_steps)
            / (jnp.sqrt(second_now / (1.0 - beta_two**adam_steps)) + adam_eps)
        )
        old = master[0, j]
        master_now = old - learn_rate * (corrected + decay_rate * old)
        new_master[0, j] = master_now
        new_moment[0, j] = moment_now
        new_second[0, j] = second_now
        rounded.append(master_now.astype(BF16))
    for sec in range(2):
        part = jnp.where(upper, rounded[1 - sec], rounded[sec])
        for i in range(4):
            shared[i, sec] = part


def finish_kernel(full, out, sem):
    upper = jnp.where(lax.axis_index("y") >= 2, 1, 0)
    copies = []
    for near in range(8):
        for zh in range(2):
            for sec in range(2):
                c = sec + upper - 2 * sec * upper
                at = (zh * 8 + near) * 384
                for p in range(2):
                    copies.append(
                        pltpu.make_async_copy(
                            full.at[near, 2 * p + zh, sec], out.at[0, c, p, :, pl.ds(at, 384)], sem
                        )
                    )
    for copy in copies:
        copy.start()
    for copy in copies:
        copy.wait()


def body(acts, grads_sent, replicas, master, moment, second):
    w_out, down, down_a, down_b, up = call(
        take_kernel,
        [((UNITS, D), BF16), ((64, D), BF16), ((48, D), BF16), ((16, D), BF16), ((64, D), BF16)],
        grads_sent, replicas, specs=[HBM, HBM],
        scratch=[pltpu.SemaphoreType.DMA((5,))], vmem=58,
    )
    from_before = shifted(up, 1, range(7))
    down = after(up, down, 10**10)
    from_after = shifted(down, -1, range(1, 7))
    w_out = after(down, w_out, 10**10)
    w_out_moved = lax.ppermute(w_out, FAR, weights_route())
    down_a = after(w_out, down_a, 10**10)
    after_a = shifted(down_a, -1, (7,))
    acts, weights = here(acts), here(replicas)
    (pre_act,) = call(forward_kernel, [((2, UNITS, 64), F32)], acts, weights, flops=10**10)
    (sent,) = call(
        wrap_kernel, [((2 * UNITS, 64), F32)], here(w_out_moved), down, up, pre_act
    )
    wrapped = lax.ppermute(sent, SECTION, wrap_route())
    down_b = after(sent, down_b, 10**10)
    after_b = shifted(down_b, -1, (7,))
    pre_act = after(down_b, pre_act, 10**10)
    keep, send = call(
        terms_kernel,
        [((4, 64, 768), F32), ((4, 64, 768), BF16)],
        here(from_after), here(after_a), here(after_b), here(from_before), here(wrapped),
        acts, weights, pre_act, down, up,
        scratch=[pltpu.VMEM((UNITS, 64), F32), pltpu.VMEM((UNITS, 64), F32)],
    )
    arrived = swap_cores(send)
    (tiles,) = call(merge_kernel, [((4, 64, 768), BF16)], keep, here(arrived))
    near = lax.all_to_all(tiles, "x", 0, 0, tiled=True)
    total, swap = call(near_kernel, [((64, 768), BF16), ((UNITS, 768), BF16)], here(near))
    swap = lax.ppermute(swap, SECTION, swap_route())
    (spread,) = call(spread_kernel, [((4, 2, UNITS, 384), BF16)], total, here(swap))
    far = lax.all_to_all(spread, FAR, 0, 0, axis_index_groups=far_groups(), tiled=True)
    shard = ((1, 2, UNITS, 384), F32)
    new_master, new_moment, new_second, shared = call(
        adam_kernel,
        [shard, shard, shard, ((4, 2, UNITS, 384), BF16)],
        here(far), here(master), here(moment), here(second),
    )
    shared = lax.all_to_all(shared, FAR, 0, 0, axis_index_groups=far_groups(), tiled=True)
    full = lax.all_gather(shared, NEAR, axis=0, tiled=False)
    (new_replicas,) = call(
        finish_kernel,
        [jax.ShapeDtypeStruct((1, 2, 2, UNITS, D), BF16)],
        here(full), scratch=[pltpu.SemaphoreType.DMA],
    )
    return (new_master, new_moment, new_second, new_replicas)


def solution(mesh):
    fine = Mesh(mesh.devices.reshape(4, 8, 2, 4, 2), ("y", "zl", "zh", "x", "c"))
    in_specs = (
        P(SECTION, None, DP, None),
        P(SECTION, None, DP, None),
        P(SECTION, None, None, None, None),
        P(SECTION, None, None, DP),
        P(SECTION, None, None, DP),
        P(SECTION, None, None, DP),
    )
    out_specs = (
        P(SECTION, None, None, DP),
        P(SECTION, None, None, DP),
        P(SECTION, None, None, DP),
        P(SECTION, None, None, None, None),
    )
    return jax.shard_map(body, mesh=fine, in_specs=in_specs, out_specs=out_specs, check_vma=False)
```

```python
import functools

import jax
import jax.numpy as jnp
from jax import lax
from jax.experimental import pallas as pl
from jax.experimental.pallas import tpu as pltpu
from jax.sharding import Mesh, PartitionSpec as P

D = 6144
FF = 24576
UNITS = 16
INV_WIDTH = 1.0 / D**0.5
INV_HIDDEN = 1.0 / FF**0.5

beta_one = 0.9
beta_two = 0.95
adam_eps = 1e-08
learn_rate = 0.05
decay_rate = 0.01
adam_steps = 10.0

SECTION = ("y", "zl")
DP = ("zh", "x", "c")
NEAR = ("x", "c")
FAR = ("y", "zl", "zh")

ANY = pl.BlockSpec(memory_space=pl.ANY)
HBM = pl.BlockSpec(memory_space=pltpu.HBM)
VMEM = pl.BlockSpec(memory_space=pltpu.VMEM)
BF16 = jnp.bfloat16
F32 = jnp.float32


def far_groups():
    groups = []
    for low in range(16):
        groups.append([w * 2 + zh for w in (low, 31 - low) for zh in range(2)])
    return groups


def wrap_route():
    route = []
    for left in range(7, 32, 8):
        right = (left + 1) % 32
        route += [(left, right), (right, left)]
    return route


def swap_route():
    return [(7, 23), (23, 7), (8, 24), (24, 8)]


def weights_route():
    route = []
    for w, v in wrap_route():
        for zh in range(2):
            route.append((w * 2 + zh, v * 2 + 1 - zh))
    return route


def shifted(block, distance, senders):
    route = [(w, (w + distance) % 32) for w in range(32) if w % 8 in senders]
    return lax.ppermute(block, SECTION, route)


def swap_cores(block):
    return lax.ppermute(block, "c", [(0, 1), (1, 0)])


def here(array):
    return pltpu.with_memory_space_constraint(array, pltpu.VMEM)


def call(kernel, outs, *args, specs=None, scratch=(), flops=0, moved=0, vmem=32):
    return pl.pallas_call(
        kernel,
        out_shape=[pltpu.VMEM(*out) if isinstance(out, tuple) else out for out in outs],
        in_specs=specs or [VMEM] * len(args),
        out_specs=[VMEM if isinstance(out, tuple) else ANY for out in outs],
        scratch_shapes=list(scratch),
        cost_estimate=pl.CostEstimate(flops=flops, bytes_accessed=moved, transcendentals=0),
        compiler_params=pltpu.CompilerParams(vmem_limit_bytes=vmem * 2**20),
    )(*args)


def gelu_exact(values):
    return 0.5 * values * (1.0 + lax.erf(values * 0.7071067811865476))


def gelu_slope(values):
    return (
        0.5 * (1.0 + lax.erf(values * 0.7071067811865476))
        + values * jnp.exp(-0.5 * values * values) * 0.3989422804014327
    )


def dot(a, b, ca, cb):
    return lax.dot_general(a, b, (((ca,), (cb,)), ((), ())), preferred_element_type=F32)


def joined(*parts):
    return jnp.concatenate([part[...] for part in parts], axis=0)


def columns(parts, at):
    return joined(*[part.at[:, at : at + 384] for part in parts])


def take_kernel(grads, weights, w_out, down, down_a, down_b, up, sems):
    side = jnp.where(lax.axis_index("zl") == 7, 0, 1)
    copies = [
        pltpu.make_async_copy(weights.at[0, side, 1], w_out, sems.at[0]),
        pltpu.make_async_copy(grads.at[0, 1], up, sems.at[1]),
        pltpu.make_async_copy(grads.at[0, 0], down, sems.at[2]),
        pltpu.make_async_copy(grads.at[0, 0, :48], down_a, sems.at[3]),
        pltpu.make_async_copy(grads.at[0, 0, 48:], down_b, sems.at[4]),
    ]
    for copy in copies:
        copy.start()
    for copy in copies:
        copy.wait()


def after_kernel(_, value, out):
    del value, out


def after(first, value, flops):
    return pl.pallas_call(
        after_kernel,
        out_shape=pltpu.VMEM(value.shape, value.dtype),
        in_specs=[VMEM, VMEM],
        out_specs=VMEM,
        input_output_aliases={1: 0},
        cost_estimate=pl.CostEstimate(flops=flops, bytes_accessed=0, transcendentals=0),
        compiler_params=pltpu.CompilerParams(vmem_limit_bytes=2 * 2**20),
    )(here(first), here(value))


def forward_kernel(acts, weights, pre_act):
    for c in range(2):
        pre_act[c] = dot(weights[0, c, 0], acts[0, c], 1, 1) * INV_WIDTH


def wrap_kernel(w_out, down, up, pre_act, sent):
    left = lax.axis_index("zl") == 7

    @pl.when(left)
    def _():
        sent[:UNITS] = pre_act[0]
        sent[UNITS:] = dot(w_out[...], up[...], 1, 1) * INV_HIDDEN

    @pl.when(jnp.logical_not(left))
    def _():
        sent[:UNITS] = pre_act[1]
        sent[UNITS:] = dot(w_out[...], down[...], 1, 1) * INV_HIDDEN


def terms_kernel(
    from_after, after_a, after_b, from_before, wrapped, acts, weights, pre_act, down, up,
    keep, send, grad, factor,
):
    zl = lax.axis_index("zl")
    first = lax.axis_index("c") == 0

    def product(lhs, rhs, scale, row):
        for block in range(8):
            x, zh = block % 4, block // 4
            even = dot(lhs, columns(rhs, block * 768), 1, 0) * scale
            odd = dot(lhs, columns(rhs, block * 768 + 384), 1, 0) * scale
            spot = (x, pl.ds(row, UNITS), pl.ds(zh * 384, 384))
            keep[spot] = jnp.where(first, even, odd)
            send[spot] = jnp.where(first, odd, even).astype(BF16)

    for c in range(2):
        wrap = zl == (7 if c == 0 else 0)
        if c == 0:
            own = up
            beside = zl == 6
            sources = [
                (jnp.logical_not(wrap | beside), (from_after,)),
                (beside, (after_a, after_b)),
            ]
        else:
            own = down
            sources = [(jnp.logical_not(wrap), (from_before,))]

        @pl.when(wrap)
        def _():
            grad[...] = wrapped[UNITS:]
            factor[...] = wrapped[:UNITS]

        for chosen, upstream in sources:

            @pl.when(chosen)
            def _():
                grad[...] = dot(weights[0, c, 1], joined(*upstream), 1, 1) * INV_HIDDEN
                factor[...] = pre_act[c]

        pre_grad = (grad[...] * gelu_slope(pre_act[c])).astype(BF16)
        activation = gelu_exact(factor[...]).astype(BF16)
        row = c * 2 * UNITS
        product(pre_grad, (acts.at[0, c],), INV_WIDTH, row)
        for chosen, upstream in [(wrap, (own,))] + sources:

            @pl.when(chosen)
            def _():
                product(activation, upstream, INV_HIDDEN, row + UNITS)


def merge_kernel(keep, arrived, out):
    out[...] = (keep[...] + arrived[...].astype(F32)).astype(BF16)


def near_kernel(arrived, total, swap):
    for row in range(4):
        rows = pl.ds(row * UNITS, UNITS)
        part = arrived[0, rows].astype(F32)
        for x in range(1, 4):
            part += arrived[x, rows].astype(F32)
        total[rows] = part.astype(BF16)
    side = jnp.where(lax.axis_index("zl") == 7, UNITS, 3 * UNITS)
    swap[...] = total[pl.ds(pl.multiple_of(side, UNITS), UNITS)]


def spread_kernel(total, swap, out):
    y, zl = lax.axis_index("y"), lax.axis_index("zl")
    upper = y >= 2
    for zh in range(2):
        columns = slice(zh * 384, zh * 384 + 384)
        for p in range(2):
            parts = []
            for c in range(2):
                part = total[(2 * c + p) * UNITS : (2 * c + p + 1) * UNITS, columns]
                if p == 1:
                    moved = (zl == (7 if c == 0 else 0)) & (y % 2 == c)
                    part = jnp.where(moved, swap[:, columns], part)
                parts.append(part)
            out[2 * p + zh, 0] = jnp.where(upper, parts[1], parts[0])
            out[2 * p + zh, 1] = jnp.where(upper, parts[0], parts[1])


def adam_kernel(arrived, master, moment, second, new_master, new_moment, new_second, shared):
    upper = lax.axis_index("y") >= 2
    sums = []
    for sec in range(2):
        part = arrived[0, sec].astype(F32)
        for i in range(1, 4):
            part += arrived[i, sec].astype(F32)
        sums.append(part)
    rounded = []
    for j in range(2):
        grad = jnp.where(upper, sums[1 - j], sums[j])
        moment_now = beta_one * moment[0, j] + (1.0 - beta_one) * grad
        second_now = beta_two * second[0, j] + (1.0 - beta_two) * grad * grad
        corrected = (
            moment_now
            / (1.0 - beta_one**adam_steps)
            / (jnp.sqrt(second_now / (1.0 - beta_two**adam_steps)) + adam_eps)
        )
        old = master[0, j]
        master_now = old - learn_rate * (corrected + decay_rate * old)
        new_master[0, j] = master_now
        new_moment[0, j] = moment_now
        new_second[0, j] = second_now
        rounded.append(master_now.astype(BF16))
    for sec in range(2):
        part = jnp.where(upper, rounded[1 - sec], rounded[sec])
        for i in range(4):
            shared[i, sec] = part


def finish_kernel(full, out, sem):
    upper = jnp.where(lax.axis_index("y") >= 2, 1, 0)
    copies = []
    for near in range(8):
        for zh in range(2):
            for sec in range(2):
                c = sec + upper - 2 * sec * upper
                at = (zh * 8 + near) * 384
                for p in range(2):
                    copies.append(
                        pltpu.make_async_copy(
                            full.at[near, 2 * p + zh, sec], out.at[0, c, p, :, pl.ds(at, 384)], sem
                        )
                    )
    for copy in copies:
        copy.start()
    for copy in copies:
        copy.wait()


def body(acts, grads_sent, replicas, master, moment, second):
    w_out, down, down_a, down_b, up = call(
        take_kernel,
        [((UNITS, D), BF16), ((64, D), BF16), ((48, D), BF16), ((16, D), BF16), ((64, D), BF16)],
        grads_sent, replicas, specs=[HBM, HBM],
        scratch=[pltpu.SemaphoreType.DMA((5,))], vmem=58,
    )
    from_before = shifted(up, 1, range(7))
    w_out = after(up, w_out, 10**10)
    w_out_moved = lax.ppermute(w_out, FAR, weights_route())
    down_a = after(w_out, down_a, 10**10)
    after_a = shifted(down_a, -1, (7,))
    down = after(down_a, down, 10**10)
    from_after = shifted(down, -1, range(1, 7))
    acts, weights = here(acts), here(replicas)
    (pre_act,) = call(forward_kernel, [((2, UNITS, 64), F32)], acts, weights, flops=10**10)
    (sent,) = call(
        wrap_kernel, [((2 * UNITS, 64), F32)], here(w_out_moved), down, up, pre_act
    )
    wrapped = lax.ppermute(sent, SECTION, wrap_route())
    down_b = after(sent, down_b, 10**10)
    after_b = shifted(down_b, -1, (7,))
    pre_act = after(down_b, pre_act, 10**10)
    keep, send = call(
        terms_kernel,
        [((4, 64, 768), F32), ((4, 64, 768), BF16)],
        here(from_after), here(after_a), here(after_b), here(from_before), here(wrapped),
        acts, weights, pre_act, down, up,
        scratch=[pltpu.VMEM((UNITS, 64), F32), pltpu.VMEM((UNITS, 64), F32)],
    )
    arrived = swap_cores(send)
    (tiles,) = call(merge_kernel, [((4, 64, 768), BF16)], keep, here(arrived))
    near = lax.all_to_all(tiles, "x", 0, 0, tiled=True)
    total, swap = call(near_kernel, [((64, 768), BF16), ((UNITS, 768), BF16)], here(near))
    swap = lax.ppermute(swap, SECTION, swap_route())
    (spread,) = call(spread_kernel, [((4, 2, UNITS, 384), BF16)], total, here(swap))
    far = lax.all_to_all(spread, FAR, 0, 0, axis_index_groups=far_groups(), tiled=True)
    shard = ((1, 2, UNITS, 384), F32)
    new_master, new_moment, new_second, shared = call(
        adam_kernel,
        [shard, shard, shard, ((4, 2, UNITS, 384), BF16)],
        here(far), here(master), here(moment), here(second),
    )
    shared = lax.all_to_all(shared, FAR, 0, 0, axis_index_groups=far_groups(), tiled=True)
    full = lax.all_gather(shared, NEAR, axis=0, tiled=False)
    (new_replicas,) = call(
        finish_kernel,
        [jax.ShapeDtypeStruct((1, 2, 2, UNITS, D), BF16)],
        here(full), scratch=[pltpu.SemaphoreType.DMA],
    )
    return (new_master, new_moment, new_second, new_replicas)


def solution(mesh):
    fine = Mesh(mesh.devices.reshape(4, 8, 2, 4, 2), ("y", "zl", "zh", "x", "c"))
    in_specs = (
        P(SECTION, None, DP, None),
        P(SECTION, None, DP, None),
        P(SECTION, None, None, None, None),
        P(SECTION, None, None, DP),
        P(SECTION, None, None, DP),
        P(SECTION, None, None, DP),
    )
    out_specs = (
        P(SECTION, None, None, DP),
        P(SECTION, None, None, DP),
        P(SECTION, None, None, DP),
        P(SECTION, None, None, None, None),
    )
    return jax.shard_map(body, mesh=fine, in_specs=in_specs, out_specs=out_specs, check_vma=False)
```

```python
import functools

import jax
import jax.numpy as jnp
from jax import lax
from jax.experimental import pallas as pl
from jax.experimental.pallas import tpu as pltpu
from jax.sharding import Mesh, PartitionSpec as P

D = 6144
FF = 24576
UNITS = 16
INV_WIDTH = 1.0 / D**0.5
INV_HIDDEN = 1.0 / FF**0.5

beta_one = 0.9
beta_two = 0.95
adam_eps = 1e-08
learn_rate = 0.05
decay_rate = 0.01
adam_steps = 10.0

SECTION = ("y", "zl")
DP = ("zh", "x", "c")
FAR = ("y", "zl", "zh")

ANY = pl.BlockSpec(memory_space=pl.ANY)
HBM = pl.BlockSpec(memory_space=pltpu.HBM)
VMEM = pl.BlockSpec(memory_space=pltpu.VMEM)
BF16 = jnp.bfloat16
F32 = jnp.float32


def far_groups():
    groups = []
    for low in range(16):
        groups.append([w * 2 + zh for w in (low, 31 - low) for zh in range(2)])
    return groups


def wrap_route():
    route = []
    for left in range(7, 32, 8):
        right = (left + 1) % 32
        route += [(left, right), (right, left)]
    return route


def swap_route():
    return [(7, 23), (23, 7), (8, 24), (24, 8)]


def weights_route():
    route = []
    for w, v in wrap_route():
        for zh in range(2):
            route.append((w * 2 + zh, v * 2 + 1 - zh))
    return route


def shifted(block, distance, senders):
    route = [(w, (w + distance) % 32) for w in range(32) if w % 8 in senders]
    return lax.ppermute(block, SECTION, route)


def both_cores(block):
    return lax.all_gather(block, "c", axis=0, tiled=False)


def here(array):
    return pltpu.with_memory_space_constraint(array, pltpu.VMEM)


def call(kernel, outs, *args, specs=None, scratch=(), flops=0, moved=0, vmem=32):
    return pl.pallas_call(
        kernel,
        out_shape=[pltpu.VMEM(*out) if isinstance(out, tuple) else out for out in outs],
        in_specs=specs or [VMEM] * len(args),
        out_specs=[VMEM if isinstance(out, tuple) else ANY for out in outs],
        scratch_shapes=list(scratch),
        cost_estimate=pl.CostEstimate(flops=flops, bytes_accessed=moved, transcendentals=0),
        compiler_params=pltpu.CompilerParams(vmem_limit_bytes=vmem * 2**20),
    )(*args)


def gelu_exact(values):
    return 0.5 * values * (1.0 + lax.erf(values * 0.7071067811865476))


def gelu_slope(values):
    return (
        0.5 * (1.0 + lax.erf(values * 0.7071067811865476))
        + values * jnp.exp(-0.5 * values * values) * 0.3989422804014327
    )


def dot(a, b, ca, cb):
    return lax.dot_general(a, b, (((ca,), (cb,)), ((), ())), preferred_element_type=F32)


def joined(*parts):
    return jnp.concatenate([part[...] for part in parts], axis=0)


def columns(parts, at):
    return joined(*[part.at[:, at : at + 384] for part in parts])


def take_kernel(grads, weights, w_out, down, down_a, down_b, up, sems):
    side = jnp.where(lax.axis_index("zl") == 7, 0, 1)
    copies = [
        pltpu.make_async_copy(weights.at[0, side, 1], w_out, sems.at[0]),
        pltpu.make_async_copy(grads.at[0, 1], up, sems.at[1]),
        pltpu.make_async_copy(grads.at[0, 0], down, sems.at[2]),
        pltpu.make_async_copy(grads.at[0, 0, :48], down_a, sems.at[3]),
        pltpu.make_async_copy(grads.at[0, 0, 48:], down_b, sems.at[4]),
    ]
    for copy in copies:
        copy.start()
    for copy in copies:
        copy.wait()


def after_kernel(_, value, out):
    del value, out


def after(first, value, flops):
    return pl.pallas_call(
        after_kernel,
        out_shape=pltpu.VMEM(value.shape, value.dtype),
        in_specs=[VMEM, VMEM],
        out_specs=VMEM,
        input_output_aliases={1: 0},
        cost_estimate=pl.CostEstimate(flops=flops, bytes_accessed=0, transcendentals=0),
        compiler_params=pltpu.CompilerParams(vmem_limit_bytes=2 * 2**20),
    )(here(first), here(value))


def forward_kernel(acts, weights, pre_act):
    for c in range(2):
        pre_act[c] = dot(weights[0, c, 0], acts[0, c], 1, 1) * INV_WIDTH


def wrap_kernel(w_out, down, up, pre_act, sent):
    left = lax.axis_index("zl") == 7

    @pl.when(left)
    def _():
        sent[:UNITS] = pre_act[0]
        sent[UNITS:] = dot(w_out[...], up[...], 1, 1) * INV_HIDDEN

    @pl.when(jnp.logical_not(left))
    def _():
        sent[:UNITS] = pre_act[1]
        sent[UNITS:] = dot(w_out[...], down[...], 1, 1) * INV_HIDDEN


def terms_kernel(
    from_after, after_a, after_b, from_before, wrapped, acts, weights, pre_act, down, up,
    keep, send, grad, factor,
):
    zl = lax.axis_index("zl")
    first = lax.axis_index("c") == 0

    def product(lhs, rhs, scale, row):
        for block in range(8):
            x, zh = block % 4, block // 4
            even = dot(lhs, columns(rhs, block * 768), 1, 0) * scale
            odd = dot(lhs, columns(rhs, block * 768 + 384), 1, 0) * scale
            spot = (x, pl.ds(row, UNITS), pl.ds(zh * 384, 384))
            keep[spot] = jnp.where(first, even, odd)
            send[spot] = jnp.where(first, odd, even).astype(BF16)

    for c in range(2):
        wrap = zl == (7 if c == 0 else 0)
        if c == 0:
            own = up
            beside = zl == 6
            sources = [
                (jnp.logical_not(wrap | beside), (from_after,)),
                (beside, (after_a, after_b)),
            ]
        else:
            own = down
            sources = [(jnp.logical_not(wrap), (from_before,))]

        @pl.when(wrap)
        def _():
            grad[...] = wrapped[UNITS:]
            factor[...] = wrapped[:UNITS]

        for chosen, upstream in sources:

            @pl.when(chosen)
            def _():
                grad[...] = dot(weights[0, c, 1], joined(*upstream), 1, 1) * INV_HIDDEN
                factor[...] = pre_act[c]

        pre_grad = (grad[...] * gelu_slope(pre_act[c])).astype(BF16)
        activation = gelu_exact(factor[...]).astype(BF16)
        row = c * 2 * UNITS
        product(pre_grad, (acts.at[0, c],), INV_WIDTH, row)
        for chosen, upstream in [(wrap, (own,))] + sources:

            @pl.when(chosen)
            def _():
                product(activation, upstream, INV_HIDDEN, row + UNITS)


def merge_kernel(keep, arrived, out):
    other = arrived[1 - lax.axis_index("c")]
    out[...] = (keep[...] + other.astype(F32)).astype(BF16)


def near_kernel(arrived, total, swap):
    for row in range(4):
        rows = pl.ds(row * UNITS, UNITS)
        part = arrived[0, rows].astype(F32)
        for x in range(1, 4):
            part += arrived[x, rows].astype(F32)
        total[rows] = part.astype(BF16)
    side = jnp.where(lax.axis_index("zl") == 7, UNITS, 3 * UNITS)
    swap[...] = total[pl.ds(pl.multiple_of(side, UNITS), UNITS)]


def spread_kernel(total, swap, out):
    y, zl = lax.axis_index("y"), lax.axis_index("zl")
    upper = y >= 2
    for zh in range(2):
        columns = slice(zh * 384, zh * 384 + 384)
        for p in range(2):
            parts = []
            for c in range(2):
                part = total[(2 * c + p) * UNITS : (2 * c + p + 1) * UNITS, columns]
                if p == 1:
                    moved = (zl == (7 if c == 0 else 0)) & (y % 2 == c)
                    part = jnp.where(moved, swap[:, columns], part)
                parts.append(part)
            out[2 * p + zh, 0] = jnp.where(upper, parts[1], parts[0])
            out[2 * p + zh, 1] = jnp.where(upper, parts[0], parts[1])


def adam_kernel(arrived, master, moment, second, new_master, new_moment, new_second, shared):
    upper = lax.axis_index("y") >= 2
    sums = []
    for sec in range(2):
        part = arrived[0, sec].astype(F32)
        for i in range(1, 4):
            part += arrived[i, sec].astype(F32)
        sums.append(part)
    rounded = []
    for j in range(2):
        grad = jnp.where(upper, sums[1 - j], sums[j])
        moment_now = beta_one * moment[0, j] + (1.0 - beta_one) * grad
        second_now = beta_two * second[0, j] + (1.0 - beta_two) * grad * grad
        corrected = (
            moment_now
            / (1.0 - beta_one**adam_steps)
            / (jnp.sqrt(second_now / (1.0 - beta_two**adam_steps)) + adam_eps)
        )
        old = master[0, j]
        master_now = old - learn_rate * (corrected + decay_rate * old)
        new_master[0, j] = master_now
        new_moment[0, j] = moment_now
        new_second[0, j] = second_now
        rounded.append(master_now.astype(BF16))
    for sec in range(2):
        part = jnp.where(upper, rounded[1 - sec], rounded[sec])
        for i in range(4):
            shared[i, sec] = part


def finish_kernel(full, out, sem):
    upper = jnp.where(lax.axis_index("y") >= 2, 1, 0)
    copies = []
    for near in range(8):
        for zh in range(2):
            for sec in range(2):
                c = sec + upper - 2 * sec * upper
                at = (zh * 8 + near) * 384
                for p in range(2):
                    copies.append(
                        pltpu.make_async_copy(
                            full.at[near % 2, near // 2, 2 * p + zh, sec], out.at[0, c, p, :, pl.ds(at, 384)], sem
                        )
                    )
    for copy in copies:
        copy.start()
    for copy in copies:
        copy.wait()


def body(acts, grads_sent, replicas, master, moment, second):
    w_out, down, down_a, down_b, up = call(
        take_kernel,
        [((UNITS, D), BF16), ((64, D), BF16), ((48, D), BF16), ((16, D), BF16), ((64, D), BF16)],
        grads_sent, replicas, specs=[HBM, HBM],
        scratch=[pltpu.SemaphoreType.DMA((5,))], vmem=58,
    )
    from_before = shifted(up, 1, range(7))
    w_out = after(up, w_out, 10**10)
    w_out_moved = lax.ppermute(w_out, FAR, weights_route())
    down_a = after(w_out, down_a, 10**10)
    after_a = shifted(down_a, -1, (7,))
    down = after(down_a, down, 10**10)
    from_after = shifted(down, -1, range(1, 7))
    acts, weights = here(acts), here(replicas)
    (pre_act,) = call(forward_kernel, [((2, UNITS, 64), F32)], acts, weights, flops=10**10)
    (sent,) = call(
        wrap_kernel, [((2 * UNITS, 64), F32)], here(w_out_moved), down, up, pre_act
    )
    wrapped = lax.ppermute(sent, SECTION, wrap_route())
    down_b = after(sent, down_b, 10**10)
    after_b = shifted(down_b, -1, (7,))
    pre_act = after(down_b, pre_act, 10**10)
    keep, send = call(
        terms_kernel,
        [((4, 64, 768), F32), ((4, 64, 768), BF16)],
        here(from_after), here(after_a), here(after_b), here(from_before), here(wrapped),
        acts, weights, pre_act, down, up,
        scratch=[pltpu.VMEM((UNITS, 64), F32), pltpu.VMEM((UNITS, 64), F32)],
    )
    arrived = both_cores(send)
    (tiles,) = call(merge_kernel, [((4, 64, 768), BF16)], keep, here(arrived))
    near = lax.all_to_all(tiles, "x", 0, 0, tiled=True)
    total, swap = call(near_kernel, [((64, 768), BF16), ((UNITS, 768), BF16)], here(near))
    swap = lax.ppermute(swap, SECTION, swap_route())
    (spread,) = call(spread_kernel, [((4, 2, UNITS, 384), BF16)], total, here(swap))
    far = lax.all_to_all(spread, FAR, 0, 0, axis_index_groups=far_groups(), tiled=True)
    shard = ((1, 2, UNITS, 384), F32)
    new_master, new_moment, new_second, shared = call(
        adam_kernel,
        [shard, shard, shard, ((4, 2, UNITS, 384), BF16)],
        here(far), here(master), here(moment), here(second),
    )
    shared = lax.all_to_all(shared, FAR, 0, 0, axis_index_groups=far_groups(), tiled=True)
    copies = jnp.broadcast_to(shared[None], (4, *shared.shape))
    full = both_cores(lax.all_to_all(copies, "x", 0, 0, tiled=True))
    (new_replicas,) = call(
        finish_kernel,
        [jax.ShapeDtypeStruct((1, 2, 2, UNITS, D), BF16)],
        here(full), scratch=[pltpu.SemaphoreType.DMA],
    )
    return (new_master, new_moment, new_second, new_replicas)


def solution(mesh):
    fine = Mesh(mesh.devices.reshape(4, 8, 2, 4, 2), ("y", "zl", "zh", "x", "c"))
    in_specs = (
        P(SECTION, None, DP, None),
        P(SECTION, None, DP, None),
        P(SECTION, None, None, None, None),
        P(SECTION, None, None, DP),
        P(SECTION, None, None, DP),
        P(SECTION, None, None, DP),
    )
    out_specs = (
        P(SECTION, None, None, DP),
        P(SECTION, None, None, DP),
        P(SECTION, None, None, DP),
        P(SECTION, None, None, None, None),
    )
    return jax.shard_map(body, mesh=fine, in_specs=in_specs, out_specs=out_specs, check_vma=False)
```

```python
import functools

import jax
import jax.numpy as jnp
from jax import lax
from jax.experimental import pallas as pl
from jax.experimental.pallas import tpu as pltpu
from jax.sharding import Mesh, PartitionSpec as P

D = 6144
FF = 24576
UNITS = 16
INV_WIDTH = 1.0 / D**0.5
INV_HIDDEN = 1.0 / FF**0.5

beta_one = 0.9
beta_two = 0.95
adam_eps = 1e-08
learn_rate = 0.05
decay_rate = 0.01
adam_steps = 10.0

SECTION = ("y", "zl")
DP = ("zh", "x", "c")
FAR = ("y", "zl", "zh")

ANY = pl.BlockSpec(memory_space=pl.ANY)
HBM = pl.BlockSpec(memory_space=pltpu.HBM)
VMEM = pl.BlockSpec(memory_space=pltpu.VMEM)
BF16 = jnp.bfloat16
F32 = jnp.float32


def far_groups():
    groups = []
    for low in range(16):
        groups.append([w * 2 + zh for w in (low, 31 - low) for zh in range(2)])
    return groups


def wrap_route():
    route = []
    for left in range(7, 32, 8):
        right = (left + 1) % 32
        route += [(left, right), (right, left)]
    return route


def swap_route():
    return [(7, 23), (23, 7), (8, 24), (24, 8)]


def weights_route():
    route = []
    for w, v in wrap_route():
        for zh in range(2):
            route.append((w * 2 + zh, v * 2 + 1 - zh))
    return route


def shifted(block, distance, senders):
    route = [(w, (w + distance) % 32) for w in range(32) if w % 8 in senders]
    return lax.ppermute(block, SECTION, route)


def both_cores(block):
    return lax.all_gather(block, "c", axis=0, tiled=False)


def here(array):
    return pltpu.with_memory_space_constraint(array, pltpu.VMEM)


def call(kernel, outs, *args, specs=None, scratch=(), flops=0, moved=0, vmem=32):
    return pl.pallas_call(
        kernel,
        out_shape=[pltpu.VMEM(*out) if isinstance(out, tuple) else out for out in outs],
        in_specs=specs or [VMEM] * len(args),
        out_specs=[VMEM if isinstance(out, tuple) else ANY for out in outs],
        scratch_shapes=list(scratch),
        cost_estimate=pl.CostEstimate(flops=flops, bytes_accessed=moved, transcendentals=0),
        compiler_params=pltpu.CompilerParams(vmem_limit_bytes=vmem * 2**20),
    )(*args)


def gelu_exact(values):
    return 0.5 * values * (1.0 + lax.erf(values * 0.7071067811865476))


def gelu_slope(values):
    return (
        0.5 * (1.0 + lax.erf(values * 0.7071067811865476))
        + values * jnp.exp(-0.5 * values * values) * 0.3989422804014327
    )


def dot(a, b, ca, cb):
    return lax.dot_general(a, b, (((ca,), (cb,)), ((), ())), preferred_element_type=F32)


def copy_all(pairs, sems):
    copies = [pltpu.make_async_copy(*pair, sems.at[i]) for i, pair in enumerate(pairs)]
    for copy in copies:
        copy.start()
    for copy in copies:
        copy.wait()


def take_kernel(grads, weights, w_out, down, up, sems):
    side = jnp.where(lax.axis_index("zl") == 7, 0, 1)
    pairs = [(weights.at[0, side, 1], w_out), (grads.at[0, 1], up), (grads.at[0, 0], down)]
    copy_all(pairs, sems)


def take_again_kernel(grads, _, down, up, sems):
    copy_all([(grads.at[0, 1], up), (grads.at[0, 0], down)], sems)


def after_kernel(_, value, out):
    del value, out


def after(first, value, flops):
    return pl.pallas_call(
        after_kernel,
        out_shape=pltpu.VMEM(value.shape, value.dtype),
        in_specs=[VMEM, VMEM],
        out_specs=VMEM,
        input_output_aliases={1: 0},
        cost_estimate=pl.CostEstimate(flops=flops, bytes_accessed=0, transcendentals=0),
        compiler_params=pltpu.CompilerParams(vmem_limit_bytes=2 * 2**20),
    )(here(first), here(value))


def forward_kernel(acts, weights, pre_act):
    for c in range(2):
        pre_act[c] = dot(weights[0, c, 0], acts[0, c], 1, 1) * INV_WIDTH


def wrap_kernel(w_out, down, up, pre_act, sent):
    left = lax.axis_index("zl") == 7

    @pl.when(left)
    def _():
        sent[:UNITS] = pre_act[0]
        sent[UNITS:] = dot(w_out[...], up[...], 1, 1) * INV_HIDDEN

    @pl.when(jnp.logical_not(left))
    def _():
        sent[:UNITS] = pre_act[1]
        sent[UNITS:] = dot(w_out[...], down[...], 1, 1) * INV_HIDDEN


def terms_kernel(
    from_after, from_left, from_before, from_right, wrapped, acts, weights, pre_act, down, up,
    keep, send, grad, factor,
):
    zl = lax.axis_index("zl")
    first = lax.axis_index("c") == 0

    def product(lhs, rhs, scale, row):
        for block in range(8):
            x, zh = block % 4, block // 4
            at = block * 768
            even = dot(lhs, rhs[:, at : at + 384], 1, 0) * scale
            odd = dot(lhs, rhs[:, at + 384 : at + 768], 1, 0) * scale
            spot = (x, pl.ds(row, UNITS), pl.ds(zh * 384, 384))
            keep[spot] = jnp.where(first, even, odd)
            send[spot] = jnp.where(first, odd, even).astype(BF16)

    for c in range(2):
        wrap = zl == (7 if c == 0 else 0)
        beside = zl == (6 if c == 0 else 1)
        sources = [
            (jnp.logical_not(wrap | beside), from_after if c == 0 else from_before),
            (beside, from_left if c == 0 else from_right),
        ]
        own = up if c == 0 else down

        @pl.when(wrap)
        def _():
            grad[...] = wrapped[UNITS:]
            factor[...] = wrapped[:UNITS]

        for chosen, upstream in sources:

            @pl.when(chosen)
            def _():
                grad[...] = dot(weights[0, c, 1], upstream[...], 1, 1) * INV_HIDDEN
                factor[...] = pre_act[c]

        pre_grad = (grad[...] * gelu_slope(pre_act[c])).astype(BF16)
        activation = gelu_exact(factor[...]).astype(BF16)
        row = c * 2 * UNITS
        product(pre_grad, acts.at[0, c], INV_WIDTH, row)
        for chosen, upstream in [(wrap, own)] + sources:

            @pl.when(chosen)
            def _():
                product(activation, upstream, INV_HIDDEN, row + UNITS)


def merge_kernel(keep, arrived, out):
    other = arrived[1 - lax.axis_index("c")]
    out[...] = (keep[...] + other.astype(F32)).astype(BF16)


def near_kernel(arrived, total, swap):
    for row in range(4):
        rows = pl.ds(row * UNITS, UNITS)
        part = arrived[0, rows].astype(F32)
        for x in range(1, 4):
            part += arrived[x, rows].astype(F32)
        total[rows] = part.astype(BF16)
    side = jnp.where(lax.axis_index("zl") == 7, UNITS, 3 * UNITS)
    swap[...] = total[pl.ds(pl.multiple_of(side, UNITS), UNITS)]


def spread_kernel(total, swap, out):
    y, zl = lax.axis_index("y"), lax.axis_index("zl")
    upper = y >= 2
    for zh in range(2):
        columns = slice(zh * 384, zh * 384 + 384)
        for p in range(2):
            parts = []
            for c in range(2):
                part = total[(2 * c + p) * UNITS : (2 * c + p + 1) * UNITS, columns]
                if p == 1:
                    moved = (zl == (7 if c == 0 else 0)) & (y % 2 == c)
                    part = jnp.where(moved, swap[:, columns], part)
                parts.append(part)
            out[2 * p + zh, 0] = jnp.where(upper, parts[1], parts[0])
            out[2 * p + zh, 1] = jnp.where(upper, parts[0], parts[1])


def adam_kernel(arrived, master, moment, second, new_master, new_moment, new_second, shared):
    upper = lax.axis_index("y") >= 2
    sums = []
    for sec in range(2):
        part = arrived[0, sec].astype(F32)
        for i in range(1, 4):
            part += arrived[i, sec].astype(F32)
        sums.append(part)
    rounded = []
    for j in range(2):
        grad = jnp.where(upper, sums[1 - j], sums[j])
        moment_now = beta_one * moment[0, j] + (1.0 - beta_one) * grad
        second_now = beta_two * second[0, j] + (1.0 - beta_two) * grad * grad
        corrected = (
            moment_now
            / (1.0 - beta_one**adam_steps)
            / (jnp.sqrt(second_now / (1.0 - beta_two**adam_steps)) + adam_eps)
        )
        old = master[0, j]
        master_now = old - learn_rate * (corrected + decay_rate * old)
        new_master[0, j] = master_now
        new_moment[0, j] = moment_now
        new_second[0, j] = second_now
        rounded.append(master_now.astype(BF16))
    for sec in range(2):
        part = jnp.where(upper, rounded[1 - sec], rounded[sec])
        for i in range(4):
            shared[i, sec] = part


def finish_kernel(full, out, sem):
    upper = jnp.where(lax.axis_index("y") >= 2, 1, 0)
    copies = []
    for near in range(8):
        for zh in range(2):
            for sec in range(2):
                c = sec + upper - 2 * sec * upper
                at = (zh * 8 + near) * 384
                for p in range(2):
                    copies.append(
                        pltpu.make_async_copy(
                            full.at[near % 2, near // 2, 2 * p + zh, sec], out.at[0, c, p, :, pl.ds(at, 384)], sem
                        )
                    )
    for copy in copies:
        copy.start()
    for copy in copies:
        copy.wait()


def body(acts, grads_sent, replicas, master, moment, second):
    block = ((64, D), BF16)
    w_out, down, up = call(
        take_kernel,
        [((UNITS, D), BF16), block, block],
        grads_sent, replicas, specs=[HBM, HBM],
        scratch=[pltpu.SemaphoreType.DMA((3,))], vmem=60,
    )
    from_right = shifted(up, 1, (0,))
    down = after(up, down, 10**10)
    from_left = shifted(down, -1, (7,))
    w_out = after(down, w_out, 10**10)
    w_out_moved = lax.ppermute(w_out, FAR, weights_route())
    down_rest, up_rest = call(
        take_again_kernel,
        [block, block],
        grads_sent, here(w_out), specs=[HBM, VMEM],
        scratch=[pltpu.SemaphoreType.DMA((2,))], vmem=56, flops=10**10,
    )
    from_before = shifted(up_rest, 1, range(1, 7))
    from_after = shifted(down_rest, -1, range(1, 7))
    acts, weights = here(acts), here(replicas)
    (pre_act,) = call(forward_kernel, [((2, UNITS, 64), F32)], acts, weights, flops=10**10)
    (sent,) = call(
        wrap_kernel, [((2 * UNITS, 64), F32)], here(w_out_moved), down, up, pre_act
    )
    wrapped = lax.ppermute(sent, SECTION, wrap_route())
    keep, send = call(
        terms_kernel,
        [((4, 64, 768), F32), ((4, 64, 768), BF16)],
        here(from_after), here(from_left), here(from_before), here(from_right), here(wrapped),
        acts, weights, pre_act, down, up,
        scratch=[pltpu.VMEM((UNITS, 64), F32), pltpu.VMEM((UNITS, 64), F32)],
    )
    arrived = both_cores(send)
    (tiles,) = call(merge_kernel, [((4, 64, 768), BF16)], keep, here(arrived))
    near = lax.all_to_all(tiles, "x", 0, 0, tiled=True)
    total, swap = call(near_kernel, [((64, 768), BF16), ((UNITS, 768), BF16)], here(near))
    swap = lax.ppermute(swap, SECTION, swap_route())
    (spread,) = call(spread_kernel, [((4, 2, UNITS, 384), BF16)], total, here(swap))
    far = lax.all_to_all(spread, FAR, 0, 0, axis_index_groups=far_groups(), tiled=True)
    shard = ((1, 2, UNITS, 384), F32)
    new_master, new_moment, new_second, shared = call(
        adam_kernel,
        [shard, shard, shard, ((4, 2, UNITS, 384), BF16)],
        here(far), here(master), here(moment), here(second),
    )
    shared = lax.all_to_all(shared, FAR, 0, 0, axis_index_groups=far_groups(), tiled=True)
    copies = jnp.broadcast_to(shared[None], (4, *shared.shape))
    full = both_cores(lax.all_to_all(copies, "x", 0, 0, tiled=True))
    (new_replicas,) = call(
        finish_kernel,
        [jax.ShapeDtypeStruct((1, 2, 2, UNITS, D), BF16)],
        here(full), scratch=[pltpu.SemaphoreType.DMA],
    )
    return (new_master, new_moment, new_second, new_replicas)


def solution(mesh):
    fine = Mesh(mesh.devices.reshape(4, 8, 2, 4, 2), ("y", "zl", "zh", "x", "c"))
    in_specs = (
        P(SECTION, None, DP, None),
        P(SECTION, None, DP, None),
        P(SECTION, None, None, None, None),
        P(SECTION, None, None, DP),
        P(SECTION, None, None, DP),
        P(SECTION, None, None, DP),
    )
    out_specs = (
        P(SECTION, None, None, DP),
        P(SECTION, None, None, DP),
        P(SECTION, None, None, DP),
        P(SECTION, None, None, None, None),
    )
    return jax.shard_map(body, mesh=fine, in_specs=in_specs, out_specs=out_specs, check_vma=False)
```

```python
import functools

import jax
import jax.numpy as jnp
from jax import lax
from jax.experimental import pallas as pl
from jax.experimental.pallas import tpu as pltpu
from jax.sharding import Mesh, PartitionSpec as P

D = 6144
FF = 24576
UNITS = 16
INV_WIDTH = 1.0 / D**0.5
INV_HIDDEN = 1.0 / FF**0.5

beta_one = 0.9
beta_two = 0.95
adam_eps = 1e-08
learn_rate = 0.05
decay_rate = 0.01
adam_steps = 10.0

SECTION = ("y", "zl")
DP = ("zh", "x", "c")
FAR = ("y", "zl", "zh")

ANY = pl.BlockSpec(memory_space=pl.ANY)
HBM = pl.BlockSpec(memory_space=pltpu.HBM)
VMEM = pl.BlockSpec(memory_space=pltpu.VMEM)
BF16 = jnp.bfloat16
F32 = jnp.float32


def far_groups():
    groups = []
    for low in range(16):
        groups.append([w * 2 + zh for w in (low, 31 - low) for zh in range(2)])
    return groups


def wrap_route():
    route = []
    for left in range(7, 32, 8):
        right = (left + 1) % 32
        route += [(left, right), (right, left)]
    return route


def swap_route():
    return [(7, 23), (23, 7), (8, 24), (24, 8)]


def weights_route():
    route = []
    for w, v in wrap_route():
        for zh in range(2):
            route.append((w * 2 + zh, v * 2 + 1 - zh))
    return route


def shifted(block, distance, senders):
    route = [(w, (w + distance) % 32) for w in range(32) if w % 8 in senders]
    return lax.ppermute(block, SECTION, route)


def both_cores(block):
    return lax.all_gather(block, "c", axis=0, tiled=False)


def here(array):
    return pltpu.with_memory_space_constraint(array, pltpu.VMEM)


def call(kernel, outs, *args, specs=None, scratch=(), flops=0, moved=0, vmem=32):
    return pl.pallas_call(
        kernel,
        out_shape=[pltpu.VMEM(*out) if isinstance(out, tuple) else out for out in outs],
        in_specs=specs or [VMEM] * len(args),
        out_specs=[VMEM if isinstance(out, tuple) else ANY for out in outs],
        scratch_shapes=list(scratch),
        cost_estimate=pl.CostEstimate(flops=flops, bytes_accessed=moved, transcendentals=0),
        compiler_params=pltpu.CompilerParams(vmem_limit_bytes=vmem * 2**20),
    )(*args)


def gelu_exact(values):
    return 0.5 * values * (1.0 + lax.erf(values * 0.7071067811865476))


def gelu_slope(values):
    return (
        0.5 * (1.0 + lax.erf(values * 0.7071067811865476))
        + values * jnp.exp(-0.5 * values * values) * 0.3989422804014327
    )


def dot(a, b, ca, cb):
    return lax.dot_general(a, b, (((ca,), (cb,)), ((), ())), preferred_element_type=F32)


def joined(*parts):
    return jnp.concatenate([part[...] for part in parts], axis=0)


def columns(parts, at):
    return joined(*[part.at[:, at : at + 384] for part in parts])


def take_kernel(grads, weights, w_out, down, down_a, down_b, up, sems):
    side = jnp.where(lax.axis_index("zl") == 7, 0, 1)
    copies = [
        pltpu.make_async_copy(weights.at[0, side, 1], w_out, sems.at[0]),
        pltpu.make_async_copy(grads.at[0, 1], up, sems.at[1]),
        pltpu.make_async_copy(grads.at[0, 0], down, sems.at[2]),
        pltpu.make_async_copy(grads.at[0, 0, :48], down_a, sems.at[3]),
        pltpu.make_async_copy(grads.at[0, 0, 48:], down_b, sems.at[4]),
    ]
    for copy in copies:
        copy.start()
    for copy in copies:
        copy.wait()


def after_kernel(_, value, out):
    del value, out


def after(first, value, flops):
    return pl.pallas_call(
        after_kernel,
        out_shape=pltpu.VMEM(value.shape, value.dtype),
        in_specs=[VMEM, VMEM],
        out_specs=VMEM,
        input_output_aliases={1: 0},
        cost_estimate=pl.CostEstimate(flops=flops, bytes_accessed=0, transcendentals=0),
        compiler_params=pltpu.CompilerParams(vmem_limit_bytes=2 * 2**20),
    )(here(first), here(value))


def forward_kernel(acts, weights, pre_act):
    for c in range(2):
        pre_act[c] = dot(weights[0, c, 0], acts[0, c], 1, 1) * INV_WIDTH


def wrap_kernel(w_out, down, up, pre_act, sent):
    left = lax.axis_index("zl") == 7

    @pl.when(left)
    def _():
        sent[:UNITS] = pre_act[0]
        sent[UNITS:] = dot(w_out[...], up[...], 1, 1) * INV_HIDDEN

    @pl.when(jnp.logical_not(left))
    def _():
        sent[:UNITS] = pre_act[1]
        sent[UNITS:] = dot(w_out[...], down[...], 1, 1) * INV_HIDDEN


def terms_kernel(
    from_after, after_a, after_b, from_before, wrapped, acts, weights, pre_act, down, up,
    keep, send, grad, factor,
):
    zl = lax.axis_index("zl")
    first = lax.axis_index("c") == 0

    def product(lhs, rhs, scale, row):
        for block in range(8):
            x, zh = block % 4, block // 4
            even = dot(lhs, columns(rhs, block * 768), 1, 0) * scale
            odd = dot(lhs, columns(rhs, block * 768 + 384), 1, 0) * scale
            spot = (x, pl.ds(row, UNITS), pl.ds(zh * 384, 384))
            keep[spot] = jnp.where(first, even, odd)
            send[spot] = jnp.where(first, odd, even).astype(BF16)

    for c in range(2):
        wrap = zl == (7 if c == 0 else 0)
        if c == 0:
            own = up
            beside = zl == 6
            sources = [
                (jnp.logical_not(wrap | beside), (from_after,)),
                (beside, (after_a, after_b)),
            ]
        else:
            own = down
            sources = [(jnp.logical_not(wrap), (from_before,))]

        @pl.when(wrap)
        def _():
            grad[...] = wrapped[UNITS:]
            factor[...] = wrapped[:UNITS]

        for chosen, upstream in sources:

            @pl.when(chosen)
            def _():
                grad[...] = dot(weights[0, c, 1], joined(*upstream), 1, 1) * INV_HIDDEN
                factor[...] = pre_act[c]

        pre_grad = (grad[...] * gelu_slope(pre_act[c])).astype(BF16)
        activation = gelu_exact(factor[...]).astype(BF16)
        row = c * 2 * UNITS
        product(pre_grad, (acts.at[0, c],), INV_WIDTH, row)
        for chosen, upstream in [(wrap, (own,))] + sources:

            @pl.when(chosen)
            def _():
                product(activation, upstream, INV_HIDDEN, row + UNITS)


def merge_kernel(keep, arrived, out):
    other = arrived[1 - lax.axis_index("c")]
    out[...] = (keep[...] + other.astype(F32)).astype(BF16)


def near_kernel(arrived, total, swap):
    for row in range(4):
        rows = pl.ds(row * UNITS, UNITS)
        part = arrived[0, rows].astype(F32)
        for x in range(1, 4):
            part += arrived[x, rows].astype(F32)
        total[rows] = part.astype(BF16)
    side = jnp.where(lax.axis_index("zl") == 7, UNITS, 3 * UNITS)
    swap[...] = total[pl.ds(pl.multiple_of(side, UNITS), UNITS)]


def spread_kernel(total, swap, out):
    y, zl = lax.axis_index("y"), lax.axis_index("zl")
    upper = y >= 2
    for zh in range(2):
        columns = slice(zh * 384, zh * 384 + 384)
        for p in range(2):
            parts = []
            for c in range(2):
                part = total[(2 * c + p) * UNITS : (2 * c + p + 1) * UNITS, columns]
                if p == 1:
                    moved = (zl == (7 if c == 0 else 0)) & (y % 2 == c)
                    part = jnp.where(moved, swap[:, columns], part)
                parts.append(part)
            out[2 * p + zh, 0] = jnp.where(upper, parts[1], parts[0])
            out[2 * p + zh, 1] = jnp.where(upper, parts[0], parts[1])


def adam_kernel(arrived, master, moment, second, new_master, new_moment, new_second, shared):
    upper = lax.axis_index("y") >= 2
    sums = []
    for sec in range(2):
        part = arrived[0, sec].astype(F32)
        for i in range(1, 4):
            part += arrived[i, sec].astype(F32)
        sums.append(part)
    rounded = []
    for j in range(2):
        grad = jnp.where(upper, sums[1 - j], sums[j])
        moment_now = beta_one * moment[0, j] + (1.0 - beta_one) * grad
        second_now = beta_two * second[0, j] + (1.0 - beta_two) * grad * grad
        corrected = (
            moment_now
            / (1.0 - beta_one**adam_steps)
            / (jnp.sqrt(second_now / (1.0 - beta_two**adam_steps)) + adam_eps)
        )
        old = master[0, j]
        master_now = old - learn_rate * (corrected + decay_rate * old)
        new_master[0, j] = master_now
        new_moment[0, j] = moment_now
        new_second[0, j] = second_now
        rounded.append(master_now.astype(BF16))
    for sec in range(2):
        part = jnp.where(upper, rounded[1 - sec], rounded[sec])
        for i in range(4):
            shared[i, sec] = part


def finish_kernel(full, out, sem):
    upper = jnp.where(lax.axis_index("y") >= 2, 1, 0)
    copies = []
    for near in range(8):
        for zh in range(2):
            for sec in range(2):
                c = sec + upper - 2 * sec * upper
                at = (zh * 8 + near) * 384
                for p in range(2):
                    copies.append(
                        pltpu.make_async_copy(
                            full.at[near, 2 * p + zh, sec], out.at[0, c, p, :, pl.ds(at, 384)], sem
                        )
                    )
    for copy in copies:
        copy.start()
    for copy in copies:
        copy.wait()


def body(acts, grads_sent, replicas, master, moment, second):
    w_out, down, down_a, down_b, up = call(
        take_kernel,
        [((UNITS, D), BF16), ((64, D), BF16), ((48, D), BF16), ((16, D), BF16), ((64, D), BF16)],
        grads_sent, replicas, specs=[HBM, HBM],
        scratch=[pltpu.SemaphoreType.DMA((5,))], vmem=58,
    )
    from_before = shifted(up, 1, range(7))
    w_out = after(up, w_out, 10**10)
    w_out_moved = lax.ppermute(w_out, FAR, weights_route())
    down_a = after(w_out, down_a, 10**10)
    after_a = shifted(down_a, -1, (7,))
    down = after(down_a, down, 10**10)
    from_after = shifted(down, -1, range(1, 7))
    acts, weights = here(acts), here(replicas)
    (pre_act,) = call(forward_kernel, [((2, UNITS, 64), F32)], acts, weights, flops=10**10)
    (sent,) = call(
        wrap_kernel, [((2 * UNITS, 64), F32)], here(w_out_moved), down, up, pre_act
    )
    wrapped = lax.ppermute(sent, SECTION, wrap_route())
    down_b = after(sent, down_b, 10**10)
    after_b = shifted(down_b, -1, (7,))
    pre_act = after(down_b, pre_act, 10**10)
    keep, send = call(
        terms_kernel,
        [((4, 64, 768), F32), ((4, 64, 768), BF16)],
        here(from_after), here(after_a), here(after_b), here(from_before), here(wrapped),
        acts, weights, pre_act, down, up,
        scratch=[pltpu.VMEM((UNITS, 64), F32), pltpu.VMEM((UNITS, 64), F32)],
    )
    arrived = both_cores(send)
    (tiles,) = call(merge_kernel, [((4, 64, 768), BF16)], keep, here(arrived))
    near = lax.all_to_all(tiles, "x", 0, 0, tiled=True)
    total, swap = call(near_kernel, [((64, 768), BF16), ((UNITS, 768), BF16)], here(near))
    swap = lax.ppermute(swap, SECTION, swap_route())
    (spread,) = call(spread_kernel, [((4, 2, UNITS, 384), BF16)], total, here(swap))
    far = lax.all_to_all(spread, FAR, 0, 0, axis_index_groups=far_groups(), tiled=True)
    shard = ((1, 2, UNITS, 384), F32)
    new_master, new_moment, new_second, shared = call(
        adam_kernel,
        [shard, shard, shard, ((4, 2, UNITS, 384), BF16)],
        here(far), here(master), here(moment), here(second),
    )
    shared = lax.all_to_all(shared, FAR, 0, 0, axis_index_groups=far_groups(), tiled=True)
    full = lax.all_gather(shared, ("x", "c"), axis=0, tiled=False)
    (new_replicas,) = call(
        finish_kernel,
        [jax.ShapeDtypeStruct((1, 2, 2, UNITS, D), BF16)],
        here(full), scratch=[pltpu.SemaphoreType.DMA],
    )
    return (new_master, new_moment, new_second, new_replicas)


def solution(mesh):
    fine = Mesh(mesh.devices.reshape(4, 8, 2, 4, 2), ("y", "zl", "zh", "x", "c"))
    in_specs = (
        P(SECTION, None, DP, None),
        P(SECTION, None, DP, None),
        P(SECTION, None, None, None, None),
        P(SECTION, None, None, DP),
        P(SECTION, None, None, DP),
        P(SECTION, None, None, DP),
    )
    out_specs = (
        P(SECTION, None, None, DP),
        P(SECTION, None, None, DP),
        P(SECTION, None, None, DP),
        P(SECTION, None, None, None, None),
    )
    return jax.shard_map(body, mesh=fine, in_specs=in_specs, out_specs=out_specs, check_vma=False)
```

```python
import functools

import jax
import jax.numpy as jnp
from jax import lax
from jax.experimental import pallas as pl
from jax.experimental.pallas import tpu as pltpu
from jax.sharding import Mesh, PartitionSpec as P

D = 6144
FF = 24576
UNITS = 16
INV_WIDTH = 1.0 / D**0.5
INV_HIDDEN = 1.0 / FF**0.5

beta_one = 0.9
beta_two = 0.95
adam_eps = 1e-08
learn_rate = 0.05
decay_rate = 0.01
adam_steps = 10.0

SECTION = ("y", "zl")
DP = ("zh", "x", "c")
FAR = ("y", "zl", "zh")

ANY = pl.BlockSpec(memory_space=pl.ANY)
HBM = pl.BlockSpec(memory_space=pltpu.HBM)
VMEM = pl.BlockSpec(memory_space=pltpu.VMEM)
BF16 = jnp.bfloat16
F32 = jnp.float32


def far_groups():
    groups = []
    for low in range(16):
        groups.append([w * 2 + zh for w in (low, 31 - low) for zh in range(2)])
    return groups


def wrap_route():
    route = []
    for left in range(7, 32, 8):
        right = (left + 1) % 32
        route += [(left, right), (right, left)]
    return route


def swap_route():
    return [(7, 23), (23, 7), (8, 24), (24, 8)]


def weights_route():
    route = []
    for w, v in wrap_route():
        for zh in range(2):
            route.append((w * 2 + zh, v * 2 + 1 - zh))
    return route


def shifted(block, distance, senders):
    route = [(w, (w + distance) % 32) for w in range(32) if w % 8 in senders]
    return lax.ppermute(block, SECTION, route)


def both_cores(block):
    return lax.all_gather(block, "c", axis=0, tiled=False)


def here(array):
    return pltpu.with_memory_space_constraint(array, pltpu.VMEM)


def call(kernel, outs, *args, specs=None, scratch=(), flops=0, moved=0, vmem=32):
    return pl.pallas_call(
        kernel,
        out_shape=[pltpu.VMEM(*out) if isinstance(out, tuple) else out for out in outs],
        in_specs=specs or [VMEM] * len(args),
        out_specs=[VMEM if isinstance(out, tuple) else ANY for out in outs],
        scratch_shapes=list(scratch),
        cost_estimate=pl.CostEstimate(flops=flops, bytes_accessed=moved, transcendentals=0),
        compiler_params=pltpu.CompilerParams(vmem_limit_bytes=vmem * 2**20),
    )(*args)


def gelu_exact(values):
    return 0.5 * values * (1.0 + lax.erf(values * 0.7071067811865476))


def gelu_slope(values):
    return (
        0.5 * (1.0 + lax.erf(values * 0.7071067811865476))
        + values * jnp.exp(-0.5 * values * values) * 0.3989422804014327
    )


def dot(a, b, ca, cb):
    return lax.dot_general(a, b, (((ca,), (cb,)), ((), ())), preferred_element_type=F32)


def joined(*parts):
    return jnp.concatenate([part[...] for part in parts], axis=0)


def columns(parts, at):
    return joined(*[part.at[:, at : at + 384] for part in parts])


def copy_all(pairs, sems):
    copies = [pltpu.make_async_copy(*pair, sems.at[i]) for i, pair in enumerate(pairs)]
    for copy in copies:
        copy.start()
    for copy in copies:
        copy.wait()


def take_kernel(grads, weights, w_out, down, down_a, down_b, up, sems):
    side = jnp.where(lax.axis_index("zl") == 7, 0, 1)
    copies = [
        pltpu.make_async_copy(weights.at[0, side, 1], w_out, sems.at[0]),
        pltpu.make_async_copy(grads.at[0, 1], up, sems.at[1]),
        pltpu.make_async_copy(grads.at[0, 0], down, sems.at[2]),
        pltpu.make_async_copy(grads.at[0, 0, :48], down_a, sems.at[3]),
        pltpu.make_async_copy(grads.at[0, 0, 48:], down_b, sems.at[4]),
    ]
    for copy in copies:
        copy.start()
    for copy in copies:
        copy.wait()


def after_kernel(_, value, out):
    del value, out


def after(first, value, flops):
    return pl.pallas_call(
        after_kernel,
        out_shape=pltpu.VMEM(value.shape, value.dtype),
        in_specs=[VMEM, VMEM],
        out_specs=VMEM,
        input_output_aliases={1: 0},
        cost_estimate=pl.CostEstimate(flops=flops, bytes_accessed=0, transcendentals=0),
        compiler_params=pltpu.CompilerParams(vmem_limit_bytes=2 * 2**20),
    )(here(first), here(value))


def forward_kernel(acts, weights, pre_act):
    for c in range(2):
        pre_act[c] = dot(weights[0, c, 0], acts[0, c], 1, 1) * INV_WIDTH


def wrap_kernel(w_out, down, up, pre_act, sent):
    left = lax.axis_index("zl") == 7

    @pl.when(left)
    def _():
        sent[:UNITS] = pre_act[0]
        sent[UNITS:] = dot(w_out[...], up[...], 1, 1) * INV_HIDDEN

    @pl.when(jnp.logical_not(left))
    def _():
        sent[:UNITS] = pre_act[1]
        sent[UNITS:] = dot(w_out[...], down[...], 1, 1) * INV_HIDDEN


def terms_kernel(
    from_after, after_a, after_b, from_before, wrapped, acts, weights, pre_act, down, up,
    keep, send, grad, factor,
):
    zl = lax.axis_index("zl")
    first = lax.axis_index("c") == 0

    def product(lhs, rhs, scale, row):
        for block in range(8):
            x, zh = block % 4, block // 4
            even = dot(lhs, columns(rhs, block * 768), 1, 0) * scale
            odd = dot(lhs, columns(rhs, block * 768 + 384), 1, 0) * scale
            spot = (x, pl.ds(row, UNITS), pl.ds(zh * 384, 384))
            keep[spot] = jnp.where(first, even, odd)
            send[spot] = jnp.where(first, odd, even).astype(BF16)

    for c in range(2):
        wrap = zl == (7 if c == 0 else 0)
        if c == 0:
            own = up
            beside = zl == 6
            sources = [
                (jnp.logical_not(wrap | beside), (from_after,)),
                (beside, (after_a, after_b)),
            ]
        else:
            own = down
            sources = [(jnp.logical_not(wrap), (from_before,))]

        @pl.when(wrap)
        def _():
            grad[...] = wrapped[UNITS:]
            factor[...] = wrapped[:UNITS]

        for chosen, upstream in sources:

            @pl.when(chosen)
            def _():
                grad[...] = dot(weights[0, c, 1], joined(*upstream), 1, 1) * INV_HIDDEN
                factor[...] = pre_act[c]

        pre_grad = (grad[...] * gelu_slope(pre_act[c])).astype(BF16)
        activation = gelu_exact(factor[...]).astype(BF16)
        row = c * 2 * UNITS
        product(pre_grad, (acts.at[0, c],), INV_WIDTH, row)
        for chosen, upstream in [(wrap, (own,))] + sources:

            @pl.when(chosen)
            def _():
                product(activation, upstream, INV_HIDDEN, row + UNITS)


def merge_kernel(keep, arrived, out):
    other = arrived[1 - lax.axis_index("c")]
    out[...] = (keep[...] + other.astype(F32)).astype(BF16)


def near_kernel(arrived, total, swap):
    for row in range(4):
        rows = pl.ds(row * UNITS, UNITS)
        part = arrived[0, rows].astype(F32)
        for x in range(1, 4):
            part += arrived[x, rows].astype(F32)
        total[rows] = part.astype(BF16)
    side = jnp.where(lax.axis_index("zl") == 7, UNITS, 3 * UNITS)
    swap[...] = total[pl.ds(pl.multiple_of(side, UNITS), UNITS)]


def spread_kernel(total, swap, out):
    y, zl = lax.axis_index("y"), lax.axis_index("zl")
    upper = y >= 2
    for zh in range(2):
        columns = slice(zh * 384, zh * 384 + 384)
        for p in range(2):
            parts = []
            for c in range(2):
                part = total[(2 * c + p) * UNITS : (2 * c + p + 1) * UNITS, columns]
                if p == 1:
                    moved = (zl == (7 if c == 0 else 0)) & (y % 2 == c)
                    part = jnp.where(moved, swap[:, columns], part)
                parts.append(part)
            out[2 * p + zh, 0] = jnp.where(upper, parts[1], parts[0])
            out[2 * p + zh, 1] = jnp.where(upper, parts[0], parts[1])


def adam_kernel(arrived, master, moment, second, new_master, new_moment, new_second, shared):
    upper = lax.axis_index("y") >= 2
    sums = []
    for sec in range(2):
        part = arrived[0, sec].astype(F32)
        for i in range(1, 4):
            part += arrived[i, sec].astype(F32)
        sums.append(part)
    rounded = []
    for j in range(2):
        grad = jnp.where(upper, sums[1 - j], sums[j])
        moment_now = beta_one * moment[0, j] + (1.0 - beta_one) * grad
        second_now = beta_two * second[0, j] + (1.0 - beta_two) * grad * grad
        corrected = (
            moment_now
            / (1.0 - beta_one**adam_steps)
            / (jnp.sqrt(second_now / (1.0 - beta_two**adam_steps)) + adam_eps)
        )
        old = master[0, j]
        master_now = old - learn_rate * (corrected + decay_rate * old)
        new_master[0, j] = master_now
        new_moment[0, j] = moment_now
        new_second[0, j] = second_now
        rounded.append(master_now.astype(BF16))
    for sec in range(2):
        part = jnp.where(upper, rounded[1 - sec], rounded[sec])
        for i in range(4):
            shared[i, sec] = part


def repeat_kernel(block, out, sems):
    copy_all([(block, out.at[i]) for i in range(4)], sems)


def finish_kernel(full, out, sem):
    upper = jnp.where(lax.axis_index("y") >= 2, 1, 0)
    copies = []
    for near in range(8):
        for zh in range(2):
            for sec in range(2):
                c = sec + upper - 2 * sec * upper
                at = (zh * 8 + near) * 384
                for p in range(2):
                    copies.append(
                        pltpu.make_async_copy(
                            full.at[near % 2, near // 2, 2 * p + zh, sec], out.at[0, c, p, :, pl.ds(at, 384)], sem
                        )
                    )
    for copy in copies:
        copy.start()
    for copy in copies:
        copy.wait()


def body(acts, grads_sent, replicas, master, moment, second):
    w_out, down, down_a, down_b, up = call(
        take_kernel,
        [((UNITS, D), BF16), ((64, D), BF16), ((48, D), BF16), ((16, D), BF16), ((64, D), BF16)],
        grads_sent, replicas, specs=[HBM, HBM],
        scratch=[pltpu.SemaphoreType.DMA((5,))], vmem=58,
    )
    from_before = shifted(up, 1, range(7))
    w_out = after(up, w_out, 10**10)
    w_out_moved = lax.ppermute(w_out, FAR, weights_route())
    down_a = after(w_out, down_a, 10**10)
    after_a = shifted(down_a, -1, (7,))
    down = after(down_a, down, 10**10)
    from_after = shifted(down, -1, range(1, 7))
    acts, weights = here(acts), here(replicas)
    (pre_act,) = call(forward_kernel, [((2, UNITS, 64), F32)], acts, weights, flops=10**10)
    (sent,) = call(
        wrap_kernel, [((2 * UNITS, 64), F32)], here(w_out_moved), down, up, pre_act
    )
    wrapped = lax.ppermute(sent, SECTION, wrap_route())
    down_b = after(sent, down_b, 10**10)
    after_b = shifted(down_b, -1, (7,))
    pre_act = after(down_b, pre_act, 10**10)
    keep, send = call(
        terms_kernel,
        [((4, 64, 768), F32), ((4, 64, 768), BF16)],
        here(from_after), here(after_a), here(after_b), here(from_before), here(wrapped),
        acts, weights, pre_act, down, up,
        scratch=[pltpu.VMEM((UNITS, 64), F32), pltpu.VMEM((UNITS, 64), F32)],
    )
    arrived = both_cores(send)
    (tiles,) = call(merge_kernel, [((4, 64, 768), BF16)], keep, here(arrived))
    near = lax.all_to_all(tiles, "x", 0, 0, tiled=True)
    total, swap = call(near_kernel, [((64, 768), BF16), ((UNITS, 768), BF16)], here(near))
    swap = lax.ppermute(swap, SECTION, swap_route())
    (spread,) = call(spread_kernel, [((4, 2, UNITS, 384), BF16)], total, here(swap))
    far = lax.all_to_all(spread, FAR, 0, 0, axis_index_groups=far_groups(), tiled=True)
    shard = ((1, 2, UNITS, 384), F32)
    new_master, new_moment, new_second, shared = call(
        adam_kernel,
        [shard, shard, shard, ((4, 2, UNITS, 384), BF16)],
        here(far), here(master), here(moment), here(second),
    )
    shared = lax.all_to_all(shared, FAR, 0, 0, axis_index_groups=far_groups(), tiled=True)
    (copies,) = call(
        repeat_kernel,
        [jax.ShapeDtypeStruct((4, *shared.shape), BF16)],
        here(shared), scratch=[pltpu.SemaphoreType.DMA((4,))],
    )
    full = both_cores(lax.all_to_all(copies, "x", 0, 0, tiled=True))
    (new_replicas,) = call(
        finish_kernel,
        [jax.ShapeDtypeStruct((1, 2, 2, UNITS, D), BF16)],
        here(full), scratch=[pltpu.SemaphoreType.DMA],
    )
    return (new_master, new_moment, new_second, new_replicas)


def solution(mesh):
    fine = Mesh(mesh.devices.reshape(4, 8, 2, 4, 2), ("y", "zl", "zh", "x", "c"))
    in_specs = (
        P(SECTION, None, DP, None),
        P(SECTION, None, DP, None),
        P(SECTION, None, None, None, None),
        P(SECTION, None, None, DP),
        P(SECTION, None, None, DP),
        P(SECTION, None, None, DP),
    )
    out_specs = (
        P(SECTION, None, None, DP),
        P(SECTION, None, None, DP),
        P(SECTION, None, None, DP),
        P(SECTION, None, None, None, None),
    )
    return jax.shard_map(body, mesh=fine, in_specs=in_specs, out_specs=out_specs, check_vma=False)
```
